512 devices in a mesh: grp: 8 (over z_lo, core), seg: 64 (over y, z_hi, x).
Axes of the slice: x: 4, y: 8, z: 8 (z_hi: 2, z_lo: 4; z = z_hi * 4 + z_lo), core: 2. Of those that a mesh axis runs over, the one named last changes fastest.
Arguments:
- queries: bfloat16 [98304, 2048], P(('seg', 'grp')), may hold values from -8 to 8
- keys: bfloat16 [98304, 2048], P(('seg', 'grp')), may hold values from -8 to 8
- values: bfloat16 [98304, 2048], P(('seg', 'grp')), may hold values from -6 to 6
- offsets_two: int32 [32], replicated, may hold values from 0 to 7
- offsets_three: int32 [32], replicated, may hold values from 0 to 63
- w_out: bfloat16 [2048, 2048], P('seg'), may hold values from -0.125 to 0.125
Outputs:
- mixed: bfloat16 [98304, 2048], P(('seg', 'grp'))
The draws below stay inside these ranges and needn't reach their ends.
All inputs are finite; a program needn't handle non-finite values.
Results may differ from the reference program's by a relative error of at most 0.0056.
Values may be sent and summed in bfloat16 or wider, within the bound.
No kernel may reach another device: no remote copies, remote signals or barrier semaphores. Data moves between devices by JAX's collectives and lax.ppermute only.
A program may use at most 128 MiB of HBM per device.

```python
import math
import jax
import jax.numpy as jnp
from jax import lax

H = 32
HD = 64
D = 2048
R2 = 8
R3 = 64
SEG1 = 1536
SEG2 = 12288
SEQ = 98304


def draw_queries(key, part):
    key = jax.random.fold_in(key, 11)
    return jnp.clip(jax.random.normal(key, (SEQ, H * HD), jnp.float32), -8.0, 8.0).astype(jnp.bfloat16)


def draw_keys(key, part):
    key = jax.random.fold_in(key, 23)
    return jnp.clip(jax.random.normal(key, (SEQ, H * HD), jnp.float32), -8.0, 8.0).astype(jnp.bfloat16)


def touch_ends(values, stream_key, smallest, high):
    extent = values.shape
    index_at = [jax.random.randint(jax.random.fold_in(stream_key, axis), (), 0, extent[axis]) for axis in range(len(extent))]
    values = values.at[tuple(index_at)].set(smallest)
    longest = extent.index(max(extent))
    index_at[longest] = (index_at[longest] + 1) % extent[longest]
    return values.at[tuple(index_at)].set(high)


def shard_levels(rng, dims, cuts, low, top_value):
    def one(axis_at, shards_of):
        heights = jax.random.uniform(jax.random.fold_in(jax.random.fold_in(rng, 6), axis_at), (shards_of,), jnp.float32, low / len(cuts), top_value / len(cuts))
        return jnp.repeat(jnp.exp(heights), dims[axis_at] // shards_of).reshape((-1,) + (1,) * (len(dims) - axis_at - 1))

    level = one(*cuts[0])
    for cut in cuts[1:]:
        level = level * one(*cut)
    return level


def normal_values(stream_key, dims, scale, limit, cuts=(), kind=jnp.bfloat16):
    level = shard_levels(stream_key, dims, cuts, -0.22, 0.18) if cuts else 1.0
    array = jax.random.normal(stream_key, dims, jnp.float32) * scale * level
    return jnp.minimum(jnp.maximum(array, -limit), limit).astype(kind)


def setup_inputs(seed: int = 0) -> dict:
    splits = jax.random.split(jax.random.key(seed), 7)
    queries = draw_queries(jax.random.fold_in(splits[6], 71), 0)
    keys = draw_keys(jax.random.fold_in(splits[6], 71), 0)
    values = normal_values(splits[2], (SEQ, D), 1.0, 6.0, ((0, 512),))
    offsets_two = touch_ends(jax.random.randint(splits[3], (H,), 0, R2), jax.random.fold_in(splits[3], 1), 0, R2 - 1).astype(jnp.int32)
    offsets_three = touch_ends(jax.random.randint(splits[4], (H,), 0, R3), jax.random.fold_in(splits[4], 1), 0, R3 - 1).astype(jnp.int32)
    w_out = normal_values(splits[5], (D, D), D ** -0.5, 0.125, ((0, 64),))
    return dict(queries=queries, keys=keys, values=values, offsets_two=offsets_two, offsets_three=offsets_three, w_out=w_out)


def attend(query_heads, key_heads, value_heads):
    count = query_heads.shape[0]
    heads = query_heads.shape[1]
    block = math.gcd(count, 512)
    scale = HD ** -0.5

    def one_head(items):
        head_q, head_k, head_v = items

        def one_block(block_q):
            scores = jnp.dot(block_q, head_k.T, preferred_element_type=jnp.float32) * scale
            largest = jnp.max(scores, axis=-1)
            expo = jnp.exp(scores - largest[:, None])
            totals = jnp.sum(expo, axis=-1)
            outputs = jnp.dot(expo.astype(jnp.bfloat16), head_v, preferred_element_type=jnp.float32) / totals[:, None]
            return largest, totals, outputs

        return lax.map(one_block, head_q.reshape(count // block, block, head_q.shape[1]))

    largest, totals, outputs = lax.map(one_head, (jnp.moveaxis(query_heads, 1, 0), jnp.moveaxis(key_heads, 1, 0), jnp.moveaxis(value_heads, 1, 0)))
    return largest.reshape(heads, count).T, totals.reshape(heads, count).T, jnp.moveaxis(outputs.reshape(heads, count, HD), 0, 1)


def choose_rows(matrix, offsets, rate):
    heads = offsets.shape[0]
    count = matrix.shape[0] // rate
    shaped = matrix.reshape(count, rate, heads, HD)
    index = jnp.broadcast_to(offsets.astype(jnp.int32)[None, None, :, None], (count, 1, heads, HD))
    return jnp.take_along_axis(shaped, index, axis=1)[:, 0]


def spread_level(level, offsets, rate):
    largest, totals, outputs = level
    count, heads = largest.shape
    row_count = count * rate
    big_largest = jnp.broadcast_to(largest[:, None], (count, rate, heads)).reshape(row_count, heads)
    big_totals = jnp.broadcast_to(totals[:, None], (count, rate, heads)).reshape(row_count, heads)
    big_outputs = jnp.broadcast_to(outputs[:, None], (count, rate, heads, HD)).reshape(row_count, heads, HD)
    cover = (jnp.arange(row_count, dtype=jnp.int32) % rate)[:, None] == offsets.astype(jnp.int32)[None, :]
    return big_largest, big_totals, big_outputs, cover


def combine(levels):
    peak = levels[0][0]
    for level in levels[1:]:
        peak = jnp.maximum(peak, jnp.where(level[3], level[0], peak))
    weight_sum = jnp.zeros_like(peak)
    summed = jnp.zeros_like(levels[0][2])
    for largest, totals, outputs, cover in levels:
        weight = jnp.where(cover, totals * jnp.exp(jnp.where(cover, largest, peak) - peak), 0.0)
        weight_sum = weight_sum + weight
        summed = summed + weight[..., None] * outputs
    return summed / weight_sum[..., None]


def reference(queries, keys, values, offsets_two, offsets_three, w_out):
    third = attend(choose_rows(queries, offsets_three, R3), choose_rows(keys, offsets_three, R3), choose_rows(values, offsets_three, R3))
    segments = SEQ // SEG2
    per_seg = SEG2 // R3
    firsts = SEG2 // SEG1

    def one_segment(items):
        seg_q, seg_k, seg_v, large_s, total_s, output_s = items
        first = lax.map(lambda block: attend(block[0], block[1], block[2]),
                        (seg_q.reshape(firsts, SEG1, H, HD), seg_k.reshape(firsts, SEG1, H, HD), seg_v.reshape(firsts, SEG1, H, HD)))
        level_one = (first[0].reshape(SEG2, H), first[1].reshape(SEG2, H), first[2].reshape(SEG2, H, HD), jnp.ones((SEG2, H), jnp.bool_))
        second = attend(choose_rows(seg_q, offsets_two, R2), choose_rows(seg_k, offsets_two, R2), choose_rows(seg_v, offsets_two, R2))
        level_two = spread_level(second, offsets_two, R2)
        level_three = spread_level((large_s, total_s, output_s), offsets_three, R3)
        attention = combine([level_one, level_two, level_three]).reshape(SEG2, D).astype(jnp.bfloat16)
        return jnp.dot(attention, w_out, preferred_element_type=jnp.float32).astype(jnp.bfloat16)

    mixed = lax.map(one_segment, (queries.reshape(segments, SEG2, D), keys.reshape(segments, SEG2, D), values.reshape(segments, SEG2, D),
                                  third[0].reshape(segments, per_seg, H), third[1].reshape(segments, per_seg, H),
                                  third[2].reshape(segments, per_seg, H, HD)))
    return mixed.reshape(SEQ, D)
```

```python
import functools
import math

import jax
import jax.numpy as jnp
from jax import lax
from jax.experimental import pallas as pl
from jax.experimental.pallas import tpu as pltpu
from jax.sharding import Mesh
from jax.sharding import PartitionSpec as P

H = 32
HD = 64
R2 = 8
R3 = 64
D = H * HD
GRP = 8
ROWS = 192
SEG1 = ROWS * GRP
OWN = H // GRP
WIDTH = OWN * HD
N2 = SEG1 // R2
N3 = SEG1 // R3
PAD3 = 32
PICK = N2 + PAD3
BLOCK = 512
SCALE2 = HD**-0.5 * math.log2(math.e)
VMEM_LIMIT = 40 * 2**20
GROUP = ("zl", "core")
NT = (((1,), (1,)), ((), ()))


def fine_mesh(mesh):
    return Mesh(mesh.devices.reshape(4, 2, 8, 2, 4), ("zl", "core", "y", "zh", "x"))


def pack_kernel(k_ref, v_ref, out_ref):
    out_ref[0, :, :WIDTH] = k_ref[...]
    out_ref[0, :, WIDTH:] = v_ref[...]


def pack(keys, values):
    block = pl.BlockSpec((ROWS, WIDTH), lambda j: (0, j))
    return pl.pallas_call(
        pack_kernel,
        grid=(GRP,),
        in_specs=[block, block],
        out_specs=pl.BlockSpec((1, ROWS, 2 * WIDTH), lambda j: (j, 0, 0)),
        out_shape=jax.ShapeDtypeStruct((GRP, ROWS, 2 * WIDTH), jnp.bfloat16),
        name="pack_kv",
    )(keys, values)


def pick_kernel(off_ref, kv_ref, out_ref):
    row = lax.broadcasted_iota(jnp.int32, (PICK, SEG1), 0)
    col = lax.broadcasted_iota(jnp.int32, (PICK, SEG1), 1)
    lane = lax.broadcasted_iota(jnp.int32, (PICK, 2 * HD), 1)
    for pair in range(OWN // 2):
        parts = []
        for parity in range(2):
            head = 2 * pair + parity
            two = row * R2 + off_ref[head]
            three = (row - N2) * R3 + off_ref[OWN + head]
            target = jnp.where(row < N2, two, jnp.where(row < N2 + N3, three, -1))
            onehot = jnp.where(col == target, 1.0, 0.0).astype(jnp.bfloat16)
            parts.append(
                [
                    jnp.dot(
                        onehot,
                        kv_ref[:, base + pair * 2 * HD : base + (pair + 1) * 2 * HD],
                        preferred_element_type=jnp.float32,
                    )
                    for base in (0, WIDTH)
                ]
            )
        for which, base in enumerate((0, WIDTH)):
            chosen = jnp.where(lane < HD, parts[0][which], parts[1][which])
            out_ref[:, base + pair * 2 * HD : base + (pair + 1) * 2 * HD] = chosen.astype(jnp.bfloat16)


def pick(offsets, kv):
    return pl.pallas_call(
        pick_kernel,
        grid_spec=pltpu.PrefetchScalarGridSpec(
            num_scalar_prefetch=1,
            grid=(1,),
            in_specs=[pl.BlockSpec((SEG1, 2 * WIDTH), lambda i, off: (0, 0))],
            out_specs=pl.BlockSpec((PICK, 2 * WIDTH), lambda i, off: (0, 0)),
        ),
        out_shape=jax.ShapeDtypeStruct((PICK, 2 * WIDTH), jnp.bfloat16),
        compiler_params=pltpu.CompilerParams(vmem_limit_bytes=VMEM_LIMIT),
        cost_estimate=pl.CostEstimate(flops=4 * 10**9, bytes_accessed=2 * 10**6, transcendentals=0),
        name="pick_rows",
    )(offsets, kv)


def soft(scores):
    largest = jnp.max(scores, axis=-1, keepdims=True)
    return largest, jnp.exp2((scores - largest) * SCALE2).astype(jnp.bfloat16)


def attention_kernel(off_ref, q_ref, k_ref, v_ref, k2_ref, v2_ref, k3_ref, v3_ref, out_ref, acc, top, aug, aug2, aug3):
    pair = pl.program_id(0)
    for parity in range(2):
        head = 2 * pair + parity

        def mine(rows):
            lane = lax.broadcasted_iota(jnp.int32, (rows, 2 * HD), 1)
            return (lane >= HD) if parity else (lane < HD)

        one = jnp.ones((), jnp.bfloat16)
        aug[...] = jnp.where(mine(SEG1), v_ref[...], one)
        aug2[...] = jnp.where(mine(aug2.shape[0]), v2_ref[...], one)
        aug3[...] = jnp.where(mine(aug3.shape[0]), v3_ref[...], one)

        def level_one(block, carry):
            rows = pl.ds(pl.multiple_of(block * BLOCK, BLOCK), BLOCK)
            own_q = jnp.where(mine(BLOCK), q_ref[rows, :], jnp.zeros((), jnp.bfloat16))
            scores = lax.dot_general(own_q, k_ref[...], NT, preferred_element_type=jnp.float32)
            largest, expo = soft(scores)
            acc[rows, :] = jnp.dot(expo, aug[...], preferred_element_type=jnp.float32)
            top[rows, :] = jnp.broadcast_to(largest, (BLOCK, 2 * HD))
            return carry

        lax.fori_loop(0, SEG1 // BLOCK, level_one, 0)

        def sparse_level(count, used, rate, offset, far_k, far_v, period, valid):
            row = lax.broadcasted_iota(jnp.int32, (count, SEG1), 0)
            col = lax.broadcasted_iota(jnp.int32, (count, SEG1), 1)
            onehot = jnp.where(col == row * rate + offset, 1.0, 0.0).astype(jnp.bfloat16)
            own_q = jnp.dot(onehot, q_ref[...], preferred_element_type=jnp.float32)
            own_q = jnp.where(mine(count), own_q, 0.0).astype(jnp.bfloat16)
            scores = lax.dot_general(own_q, far_k[...], NT, preferred_element_type=jnp.float32)
            place = lax.broadcasted_iota(jnp.int32, (1, scores.shape[1]), 1)
            scores = jnp.where(lax.rem(place, period) < valid, scores, -1e30)
            largest, expo = soft(scores)
            part = jnp.dot(expo, far_v[...], preferred_element_type=jnp.float32)[:used]
            largest = jnp.broadcast_to(largest[:used], (used, 2 * HD))
            rows = pl.ds(offset, used, stride=rate)
            old_top = top[rows, :]
            peak = jnp.maximum(old_top, largest)
            top[rows, :] = peak
            acc[rows, :] = acc[rows, :] * jnp.exp2((old_top - peak) * SCALE2) + part * jnp.exp2((largest - peak) * SCALE2)

        sparse_level(N2, N2, R2, off_ref[head], k2_ref, aug2, PICK, N2)
        sparse_level(PAD3, N3, R3, off_ref[OWN + head], k3_ref, aug3, PAD3, N3)
        full = acc[...]
        result = (full / pltpu.roll(full, HD, 1)).astype(jnp.bfloat16)
        if parity == 0:
            out_ref[...] = result
        else:
            out_ref[...] = jnp.where(mine(SEG1), result, out_ref[...])


def attend(offsets, q, kv, far_two, far_three):
    pairs = OWN // 2

    def spec(rows, shift):
        return pl.BlockSpec((rows, 2 * HD), lambda i, off: (0, i + shift))

    rows2, rows3 = far_two.shape[0], far_three.shape[0]
    return pl.pallas_call(
        attention_kernel,
        grid_spec=pltpu.PrefetchScalarGridSpec(
            num_scalar_prefetch=1,
            grid=(pairs,),
            in_specs=[
                spec(SEG1, 0),
                spec(SEG1, 0),
                spec(SEG1, pairs),
                spec(rows2, 0),
                spec(rows2, pairs),
                spec(rows3, 0),
                spec(rows3, pairs),
            ],
            out_specs=spec(SEG1, 0),
            scratch_shapes=[
                pltpu.VMEM((SEG1, 2 * HD), jnp.float32),
                pltpu.VMEM((SEG1, 2 * HD), jnp.float32),
                pltpu.VMEM((SEG1, 2 * HD), jnp.bfloat16),
                pltpu.VMEM((rows2, 2 * HD), jnp.bfloat16),
                pltpu.VMEM((rows3, 2 * HD), jnp.bfloat16),
            ],
        ),
        out_shape=jax.ShapeDtypeStruct((SEG1, WIDTH), jnp.bfloat16),
        compiler_params=pltpu.CompilerParams(vmem_limit_bytes=VMEM_LIMIT),
        cost_estimate=pl.CostEstimate(flops=20 * 10**9, bytes_accessed=8 * 10**6, transcendentals=10**7),
        name="attend_levels",
    )(offsets, q, kv, kv, far_two, far_two, far_three, far_three)


def project_kernel(att_ref, w_ref, out_ref):
    total = jnp.dot(att_ref[0], w_ref[0, :WIDTH], preferred_element_type=jnp.float32)
    for g in range(1, GRP):
        total += jnp.dot(att_ref[g], w_ref[0, g * WIDTH : (g + 1) * WIDTH], preferred_element_type=jnp.float32)
    out_ref[...] = total.astype(jnp.bfloat16)


def project(att, w_halves):
    columns = 512
    per_half = w_halves.shape[2] // columns
    return pl.pallas_call(
        project_kernel,
        grid=(D // columns,),
        in_specs=[
            pl.BlockSpec((GRP, ROWS, WIDTH), lambda j: (0, 0, 0)),
            pl.BlockSpec((1, D, columns), lambda j: (j // per_half, 0, j % per_half)),
        ],
        out_specs=pl.BlockSpec((ROWS, columns), lambda j: (0, j)),
        out_shape=jax.ShapeDtypeStruct((ROWS, D), jnp.bfloat16),
        compiler_params=pltpu.CompilerParams(vmem_limit_bytes=VMEM_LIMIT),
        cost_estimate=pl.CostEstimate(flops=2 * ROWS * D * D, bytes_accessed=10 * 10**6, transcendentals=0),
        name="project",
    )(att, w_halves)


def gather_weights(w_rows):
    half = D // 2
    core = lax.axis_index("core")
    mine = lax.dynamic_slice_in_dim(w_rows, core * half, half, axis=1)
    both = lax.all_gather(mine, "zh", axis=0, tiled=False)
    line = lax.all_gather(both, "x", axis=1, tiled=False)
    line = line.reshape(WIDTH, half)
    columns = lax.all_gather(line, "y", axis=0, tiled=True)
    return lax.all_gather(columns, "core", axis=0, tiled=False)


def local(queries, keys, values, offsets_two, offsets_three, w_out):
    first_head = lax.axis_index(GROUP) * OWN
    offsets = jnp.concatenate(
        [
            lax.dynamic_slice_in_dim(offsets_two, first_head, OWN),
            lax.dynamic_slice_in_dim(offsets_three, first_head, OWN),
        ]
    )
    exchange = functools.partial(lax.all_to_all, axis_name=GROUP, split_axis=0, concat_axis=0, tiled=True)
    kv = exchange(pack(keys, values)).reshape(SEG1, 2 * WIDTH)
    q = exchange(jnp.swapaxes(queries.reshape(ROWS, GRP, WIDTH), 0, 1)).reshape(SEG1, WIDTH)
    picked = pick(offsets, kv)
    other = lax.ppermute(picked, "zh", [(0, 1), (1, 0)])
    far_two = lax.all_gather(jnp.concatenate([picked, other], 0), "x", axis=0, tiled=True)
    near_three = far_two.reshape(8, PICK, 2 * WIDTH)[:, N2:].reshape(8 * PAD3, 2 * WIDTH)
    far_three = lax.all_gather(near_three, "y", axis=0, tiled=True)
    att = attend(offsets, q, kv, far_two, far_three)
    att = exchange(att.reshape(GRP, ROWS, WIDTH))
    return project(att, gather_weights(w_out))


def solution(mesh):
    rows = P(("y", "zh", "x", "zl", "core"), None)
    return jax.shard_map(
        local,
        mesh=fine_mesh(mesh),
        in_specs=(rows, rows, rows, P(), P(), P(("y", "zh", "x"), None)),
        out_specs=rows,
        check_vma=False,
    )
```

```python
import functools
import math

import jax
import jax.numpy as jnp
from jax import lax
from jax.experimental import pallas as pl
from jax.experimental.pallas import tpu as pltpu
from jax.sharding import Mesh
from jax.sharding import PartitionSpec as P

H = 32
HD = 64
PAIR = 2 * HD
R2 = 8
R3 = 64
D = H * HD
GRP = 8
XS = 4
ROWS = 192
SEG1 = ROWS * GRP
OWN = H // GRP
WIDTH = OWN * HD
LOCAL2 = ROWS // R2
LOCAL3 = ROWS // R3
PICK = 32
SENT = PICK + PICK // 2
BLOCK = 256
SCALE2 = HD**-0.5 * math.log2(math.e)
VMEM_LIMIT = 40 * 2**20
GROUP = ("zl", "core")
NT = (((1,), (1,)), ((), ()))
BF16 = jnp.bfloat16
F32 = jnp.float32


def fine_mesh(mesh):
    return Mesh(mesh.devices.reshape(4, 2, 8, 2, XS), ("zl", "core", "y", "zh", "x"))


def params():
    return pltpu.CompilerParams(vmem_limit_bytes=VMEM_LIMIT)


def cost(flops, traffic, transcendentals=0):
    return pl.CostEstimate(flops=flops, bytes_accessed=traffic, transcendentals=transcendentals)


def iota(shape, dim):
    return lax.broadcasted_iota(jnp.int32, shape, dim)


def pack_kernel(two_ref, three_ref, q_ref, k_ref, v_ref, first_ref, second_ref, small_ref):
    step = pl.program_id(0)
    columns = pl.ds(pl.multiple_of(step * WIDTH, WIDTH), WIDTH)
    for pair, out_ref in enumerate((first_ref, second_ref)):
        narrow = pl.ds(pl.multiple_of(step * WIDTH + pair * PAIR, PAIR), PAIR)
        for which, ref in enumerate((q_ref, k_ref, v_ref)):
            out_ref[0, :, which * PAIR : (which + 1) * PAIR] = ref[:, narrow]
    row = iota((OWN * PICK, ROWS), 0)
    place = row % PICK
    target = jnp.full((OWN * PICK, ROWS), -1, jnp.int32)
    for i in range(OWN):
        two = place * R2 + two_ref[step * OWN + i]
        three = (place - LOCAL2) * R3 + three_ref[step * OWN + i]
        own = jnp.where(place < LOCAL2, two, jnp.where(place < LOCAL2 + LOCAL3, three, -1))
        target = jnp.where(row // PICK == i, own, target)
    onehot = jnp.where(iota((OWN * PICK, ROWS), 1) == target, 1.0, 0.0).astype(BF16)
    picked = [jnp.dot(onehot, ref[:, columns], preferred_element_type=F32) for ref in (q_ref, k_ref, v_ref)]
    low = iota((PICK, PAIR), 1) < HD
    for i in range(OWN):
        rows, lanes = slice(i * PICK, (i + 1) * PICK), slice(i // 2 * PAIR, (i // 2 + 1) * PAIR)
        q, k, v = (part[rows, lanes] for part in picked)
        if i % 2:
            k = pltpu.roll(k, HD, 1)
            head, tail = pltpu.roll(q[: PICK // 2], HD, 1), q[PICK // 2 :]
        else:
            v = pltpu.roll(v, HD, 1)
            head, tail = q[: PICK // 2], pltpu.roll(q[PICK // 2 :], HD, 1)
        small_ref[i, :PICK, :] = jnp.where(low, k, v).astype(BF16)
        small_ref[i, PICK:, :] = jnp.where(low[: PICK // 2], head, tail).astype(BF16)


def pack(offsets_two, offsets_three, queries, keys, values):
    whole = pl.BlockSpec((ROWS, D), lambda j, *_: (0, 0))
    chunk = pl.BlockSpec((1, ROWS, 3 * PAIR), lambda j, *_: (j, 0, 0))
    chunk_shape = jax.ShapeDtypeStruct((GRP, ROWS, 3 * PAIR), BF16)
    return pl.pallas_call(
        pack_kernel,
        grid_spec=pltpu.PrefetchScalarGridSpec(
            num_scalar_prefetch=2,
            grid=(GRP,),
            in_specs=[whole] * 3,
            out_specs=[chunk, chunk, pl.BlockSpec((OWN, SENT, PAIR), lambda j, *_: (j, 0, 0))],
        ),
        out_shape=[chunk_shape, chunk_shape, jax.ShapeDtypeStruct((H, SENT, PAIR), BF16)],
        compiler_params=params(),
        cost_estimate=cost(10**9, 5 * 10**6),
        name="pack",
    )(offsets_two, offsets_three, queries, keys, values)


def compact_kernel(own_ref, other_ref, out_ref):
    count = H * LOCAL3
    row = iota((count, H * PICK), 0)
    target = row // LOCAL3 * PICK + LOCAL2 + row % LOCAL3
    onehot = jnp.where(iota((count, H * PICK), 1) == target, 1.0, 0.0).astype(BF16)
    for which, ref in enumerate((own_ref, other_ref)):
        chosen = jnp.dot(onehot, ref[...], preferred_element_type=F32)
        out_ref[which * count : (which + 1) * count, :] = chosen.astype(BF16)


def compact(own, other):
    return pl.pallas_call(
        compact_kernel,
        out_shape=jax.ShapeDtypeStruct((2 * H * LOCAL3, PAIR), BF16),
        compiler_params=params(),
        cost_estimate=cost(10**8, 10**6),
        name="compact_three",
    )(own, other)


def sparse_kernel(place_ref, got_ref, other_ref, far_ref, out_ref):
    low = iota((1, PAIR), 1) < HD
    zero, one = jnp.zeros((), BF16), jnp.ones((), BF16)
    own = got_ref[:, :PICK, :].reshape(H * PICK, PAIR)
    other = other_ref[...].reshape(H * PICK, PAIR)
    far = far_ref[...]
    half = PICK // 2
    raw = got_ref[:, PICK:, :].reshape(H * half, PAIR).astype(F32)
    head = jnp.where(low, raw, 0.0)
    tail = jnp.where(low, pltpu.roll(raw, HD, 1), 0.0).reshape(H, half, PAIR)
    tail_two = tail[:, : LOCAL2 - half].reshape(-1, PAIR)
    tail_three = tail[:, LOCAL2 - half :].reshape(-1, PAIR)

    def attend(q, sets):
        q = q.astype(BF16)
        scores = []
        for kv, masked in sets:
            part = lax.dot_general(q, kv, NT, preferred_element_type=F32)
            if masked:
                part = jnp.where(iota((1, kv.shape[0]), 1) % PICK < LOCAL2, part, -1e30)
            scores.append(part)
        largest = functools.reduce(jnp.maximum, [jnp.max(part, axis=-1, keepdims=True) for part in scores])
        total = None
        for (kv, _), part in zip(sets, scores):
            expo = jnp.exp2((part - largest) * SCALE2).astype(BF16)
            part = jnp.dot(expo, jnp.where(low, one, kv), preferred_element_type=F32)
            total = part if total is None else total + part
        weight = total[:, :1]
        log_sum = largest * SCALE2 + jnp.log2(weight)
        top = log_sum.astype(BF16).astype(F32)
        middle = (log_sum - top).astype(BF16).astype(F32)
        rest = log_sum - top - middle
        lane = iota((1, PAIR), 1)
        stats = jnp.where(lane < 16, top, jnp.where(lane < 32, middle, rest))
        return jnp.where(low, stats, total / weight)

    two = ((own, True), (other, True))
    rows = H * half // 2
    first = jnp.concatenate([attend(head[:rows], two), attend(head[rows:], two)], 0)
    first = first.reshape(GRP, XS, half, PAIR)
    second = attend(tail_two, two).reshape(GRP, XS, LOCAL2 - half, PAIR)
    third = attend(tail_three, ((far, False),)).reshape(GRP, XS, PICK - LOCAL2, PAIR)
    second = jnp.concatenate([second, third], axis=2)
    for x in range(XS):
        where = (x - place_ref[0] + XS) % XS
        out_ref[where, :, :half, :] = first[:, x].astype(BF16)
        out_ref[where, :, half:, :] = second[:, x].astype(BF16)


def sparse_levels(place, got, other, far):
    shape = (XS, GRP, PICK, PAIR)
    return pl.pallas_call(
        sparse_kernel,
        in_specs=[pl.BlockSpec(memory_space=pltpu.SMEM)] + [pl.BlockSpec(memory_space=pltpu.VMEM)] * 3,
        out_shape=jax.ShapeDtypeStruct(shape, BF16),
        compiler_params=params(),
        cost_estimate=cost(4 * 10**9, 2 * 10**6, 2 * 10**6),
        name="sparse_levels",
    )(place, got, other, far)


def dense_kernel(head, scalar_ref, qkv_ref, back_ref, out_ref, acc, top, aug, few):
    zero, one = jnp.zeros((), BF16), jnp.ones((), BF16)

    def mine(parity, rows):
        lane = iota((rows, PAIR), 1)
        return (lane >= HD) if parity else (lane < HD)

    for parity in range(2):
        aug[parity] = jnp.where(mine(parity, SEG1), qkv_ref[:, 2 * PAIR :], one)

    def level_one(block, carry):
        rows = pl.ds(pl.multiple_of(block * BLOCK, BLOCK), BLOCK)
        q = qkv_ref[rows, :PAIR]
        scores = [
            lax.dot_general(
                jnp.where(mine(parity, BLOCK), q, zero), qkv_ref[:, PAIR : 2 * PAIR], NT, preferred_element_type=F32
            )
            for parity in range(2)
        ]
        for parity in range(2):
            largest = jnp.max(scores[parity], axis=-1, keepdims=True)
            expo = jnp.exp2((scores[parity] - largest) * SCALE2).astype(BF16)
            acc[parity, rows, :] = jnp.dot(expo, aug[parity], preferred_element_type=F32)
            top[parity, rows, :] = jnp.broadcast_to(largest * SCALE2, (BLOCK, PAIR))
        return carry

    lax.fori_loop(0, SEG1 // BLOCK, level_one, 0)

    for parity in range(2):
        back = back_ref[(scalar_ref[0] - head - parity + XS) % XS].astype(F32)

        def merge(rows, part, parity=parity):
            log_sum = part[:, 0:1] + part[:, 16:17] + part[:, 32:33]
            shaped = part if parity else pltpu.roll(part, HD, 1)
            shaped = jnp.where(mine(parity, part.shape[0]), shaped, 1.0)
            old = top[parity, rows, :]
            peak = jnp.maximum(old, log_sum)
            top[parity, rows, :] = peak
            acc[parity, rows, :] = acc[parity, rows, :] * jnp.exp2(old - peak) + shaped * jnp.exp2(log_sum - peak)

        two = scalar_ref[1 + parity]
        merge(pl.ds(two, SEG1 // R2, stride=R2), back[:, :LOCAL2].reshape(SEG1 // R2, PAIR))
        for g in range(GRP):
            few[g * LOCAL3 : (g + 1) * LOCAL3, :] = back[g, LOCAL2 : LOCAL2 + LOCAL3]
        three = scalar_ref[3 + parity]
        merge(pl.ds(three, SEG1 // R3, stride=R3), few[...])
    result = [acc[parity] / pltpu.roll(acc[parity], HD, 1) for parity in range(2)]
    out_ref[...] = jnp.where(mine(0, SEG1), result[0], result[1]).astype(BF16)


def dense_level(head, scalars, qkv, back):
    return pl.pallas_call(
        functools.partial(dense_kernel, head),
        in_specs=[pl.BlockSpec(memory_space=pltpu.SMEM)] + [pl.BlockSpec(memory_space=pltpu.VMEM)] * 2,
        out_shape=jax.ShapeDtypeStruct((SEG1, PAIR), BF16),
        scratch_shapes=[
            pltpu.VMEM((2, SEG1, PAIR), F32),
            pltpu.VMEM((2, SEG1, PAIR), F32),
            pltpu.VMEM((2, SEG1, PAIR), BF16),
            pltpu.VMEM((SEG1 // R3, PAIR), F32),
        ],
        compiler_params=params(),
        cost_estimate=cost(10 * 10**9, 4 * 10**6, 5 * 10**6),
        name="dense_level",
    )(scalars, qkv, back)


def project_kernel(first_ref, second_ref, w_ref, out_ref):
    part = D // H // 2
    total = None
    for g in range(GRP):
        weights = [w_ref[0, g * WIDTH + (x * 2 + zh) * part : g * WIDTH + (x * 2 + zh + 1) * part] for zh in range(2) for x in range(XS)]
        att = jnp.concatenate([first_ref[g], second_ref[g]], axis=1)
        term = jnp.dot(att, jnp.concatenate(weights, 0), preferred_element_type=F32)
        total = term if total is None else total + term
    out_ref[...] = total.astype(BF16)


def project(first, second, w_halves):
    columns = 512
    per_half = D // 2 // columns
    att = pl.BlockSpec((GRP, ROWS, PAIR), lambda j: (0, 0, 0))
    return pl.pallas_call(
        project_kernel,
        grid=(D // columns,),
        in_specs=[att, att, pl.BlockSpec((1, D, columns), lambda j: (j // per_half, 0, j % per_half))],
        out_specs=pl.BlockSpec((ROWS, columns), lambda j: (0, j)),
        out_shape=jax.ShapeDtypeStruct((ROWS, D), BF16),
        compiler_params=pltpu.CompilerParams(vmem_limit_bytes=56 * 2**20),
        cost_estimate=cost(2 * ROWS * D * D, 10 * 10**6),
        name="project",
    )(first, second, w_halves)


def swap(value):
    return lax.ppermute(value, "zh", [(0, 1), (1, 0)])


def after(value, *events):
    return lax.optimization_barrier((value, *events))[0]


def local(queries, keys, values, offsets_two, offsets_three, w_out):
    half = D // 2
    exchange = functools.partial(lax.all_to_all, axis_name=GROUP, split_axis=0, concat_axis=0, tiled=True)
    x = lax.axis_index("x")
    first_head = lax.axis_index(GROUP) * OWN
    own_two = lax.dynamic_slice_in_dim(offsets_two, first_head, OWN)
    own_three = lax.dynamic_slice_in_dim(offsets_three, first_head, OWN)

    chunk_a, chunk_b, small = pack(offsets_two, offsets_three, queries, keys, values)
    got = lax.all_to_all(small, ("zl", "core", "x"), split_axis=0, concat_axis=0, tiled=True)
    w_own = lax.dynamic_slice_in_dim(w_out, lax.axis_index("core") * half, half, axis=1)
    w_other = swap(w_own)
    upper = lax.axis_index("zh") == 1
    w_both = jnp.concatenate([jnp.where(upper, w_other, w_own), jnp.where(upper, w_own, w_other)], 0)
    w_columns = lax.all_gather(w_both, ("y", "x"), axis=0, tiled=True)

    own = got[:, :PICK]
    other = swap(own)
    qkv_a = exchange(after(chunk_a, got)).reshape(SEG1, 3 * PAIR)
    far = lax.all_gather(compact(own.reshape(H * PICK, PAIR), other.reshape(H * PICK, PAIR)), "y", axis=0, tiled=True)
    parts = sparse_levels(x.reshape(1), got, other, far)
    back = [parts[0]]
    for step in range(1, XS):
        back.append(lax.ppermute(parts[step], "x", [(i, (i + step) % XS) for i in range(XS)]))
    back = jnp.stack(back)
    qkv_b = exchange(after(chunk_b, qkv_a)).reshape(SEG1, 3 * PAIR)

    def scalars(head):
        return jnp.concatenate([x.reshape(1), own_two[head : head + 2], own_three[head : head + 2]])

    att_a = dense_level(0, scalars(0), qkv_a, back)
    w_halves = lax.all_gather(after(w_columns, qkv_b), "core", axis=0, tiled=False)
    att_b = dense_level(2, scalars(2), qkv_b, back)
    out_a = exchange(after(att_a, qkv_b).reshape(GRP, ROWS, PAIR))
    out_b = exchange(att_b.reshape(GRP, ROWS, PAIR))
    return project(out_a, out_b, w_halves)


def solution(mesh):
    rows = P(("y", "zh", "x", "zl", "core"), None)
    return jax.shard_map(
        local,
        mesh=fine_mesh(mesh),
        in_specs=(rows, rows, rows, P(), P(), P(("y", "zh", "x"), None)),
        out_specs=rows,
        check_vma=False,
    )
```

```python
import functools
import math

import jax
import jax.numpy as jnp
from jax import lax
from jax.experimental import pallas as pl
from jax.experimental.pallas import tpu as pltpu
from jax.sharding import Mesh
from jax.sharding import PartitionSpec as P

H = 32
HD = 64
PAIR = 2 * HD
R2 = 8
R3 = 64
D = H * HD
GRP = 8
XS = 4
ROWS = 192
SEG1 = ROWS * GRP
OWN = H // GRP
WIDTH = OWN * HD
LOCAL2 = ROWS // R2
LOCAL3 = ROWS // R3
PICK = 32
BULK = PAIR + 2 * WIDTH
SENT = PICK + PICK // 2
BLOCK = 256
SCALE2 = HD**-0.5 * math.log2(math.e)
VMEM_LIMIT = 40 * 2**20
GROUP = ("zl", "core")
NT = (((1,), (1,)), ((), ()))
BF16 = jnp.bfloat16
F32 = jnp.float32


def fine_mesh(mesh):
    return Mesh(mesh.devices.reshape(4, 2, 8, 2, XS), ("zl", "core", "y", "zh", "x"))


def params():
    return pltpu.CompilerParams(vmem_limit_bytes=VMEM_LIMIT)


def cost(flops, traffic, transcendentals=0):
    return pl.CostEstimate(flops=flops, bytes_accessed=traffic, transcendentals=transcendentals)


def iota(shape, dim):
    return lax.broadcasted_iota(jnp.int32, shape, dim)


def pack_kernel(two_ref, three_ref, q_ref, k_ref, v_ref, first_ref, second_ref, small_ref):
    step = pl.program_id(0)
    columns = pl.ds(pl.multiple_of(step * WIDTH, WIDTH), WIDTH)
    first_ref[0, :, :PAIR] = q_ref[:, pl.ds(pl.multiple_of(step * WIDTH, PAIR), PAIR)]
    first_ref[0, :, PAIR : PAIR + WIDTH] = k_ref[:, columns]
    first_ref[0, :, PAIR + WIDTH :] = v_ref[:, columns]
    second_ref[0] = q_ref[:, pl.ds(pl.multiple_of(step * WIDTH + PAIR, PAIR), PAIR)]
    row = iota((OWN * PICK, ROWS), 0)
    place = row % PICK
    target = jnp.full((OWN * PICK, ROWS), -1, jnp.int32)
    for i in range(OWN):
        two = place * R2 + two_ref[step * OWN + i]
        three = (place - LOCAL2) * R3 + three_ref[step * OWN + i]
        own = jnp.where(place < LOCAL2, two, jnp.where(place < LOCAL2 + LOCAL3, three, -1))
        target = jnp.where(row // PICK == i, own, target)
    onehot = jnp.where(iota((OWN * PICK, ROWS), 1) == target, 1.0, 0.0).astype(BF16)
    picked = [jnp.dot(onehot, ref[:, columns], preferred_element_type=F32) for ref in (q_ref, k_ref, v_ref)]
    low = iota((PICK, PAIR), 1) < HD
    for i in range(OWN):
        rows, lanes = slice(i * PICK, (i + 1) * PICK), slice(i // 2 * PAIR, (i // 2 + 1) * PAIR)
        q, k, v = (part[rows, lanes] for part in picked)
        if i % 2:
            k = pltpu.roll(k, HD, 1)
            head, tail = pltpu.roll(q[: PICK // 2], HD, 1), q[PICK // 2 :]
        else:
            v = pltpu.roll(v, HD, 1)
            head, tail = q[: PICK // 2], pltpu.roll(q[PICK // 2 :], HD, 1)
        small_ref[i, :PICK, :] = jnp.where(low, k, v).astype(BF16)
        small_ref[i, PICK:, :] = jnp.where(low[: PICK // 2], head, tail).astype(BF16)


def pack(offsets_two, offsets_three, queries, keys, values):
    whole = pl.BlockSpec((ROWS, D), lambda j, *_: (0, 0))

    def chunk(columns):
        return pl.BlockSpec((1, ROWS, columns), lambda j, *_: (j, 0, 0))

    def chunk_shape(columns):
        return jax.ShapeDtypeStruct((GRP, ROWS, columns), BF16)

    return pl.pallas_call(
        pack_kernel,
        grid_spec=pltpu.PrefetchScalarGridSpec(
            num_scalar_prefetch=2,
            grid=(GRP,),
            in_specs=[whole] * 3,
            out_specs=[chunk(BULK), chunk(PAIR), pl.BlockSpec((OWN, SENT, PAIR), lambda j, *_: (j, 0, 0))],
        ),
        out_shape=[chunk_shape(BULK), chunk_shape(PAIR), jax.ShapeDtypeStruct((H, SENT, PAIR), BF16)],
        compiler_params=pltpu.CompilerParams(vmem_limit_bytes=56 * 2**20),
        cost_estimate=cost(10**9, 5 * 10**6),
        name="pack",
    )(offsets_two, offsets_three, queries, keys, values)


def compact_kernel(own_ref, other_ref, out_ref):
    count = H * LOCAL3
    row = iota((count, H * PICK), 0)
    target = row // LOCAL3 * PICK + LOCAL2 + row % LOCAL3
    onehot = jnp.where(iota((count, H * PICK), 1) == target, 1.0, 0.0).astype(BF16)
    for which, ref in enumerate((own_ref, other_ref)):
        chosen = jnp.dot(onehot, ref[...], preferred_element_type=F32)
        out_ref[which * count : (which + 1) * count, :] = chosen.astype(BF16)


def compact(own, other):
    return pl.pallas_call(
        compact_kernel,
        out_shape=jax.ShapeDtypeStruct((2 * H * LOCAL3, PAIR), BF16),
        compiler_params=params(),
        cost_estimate=cost(10**8, 10**6),
        name="compact_three",
    )(own, other)


def sparse_kernel(place_ref, got_ref, other_ref, far_ref, out_ref):
    low = iota((1, PAIR), 1) < HD
    zero, one = jnp.zeros((), BF16), jnp.ones((), BF16)
    own = got_ref[:, :PICK, :].reshape(H * PICK, PAIR)
    other = other_ref[...].reshape(H * PICK, PAIR)
    far = far_ref[...]
    half = PICK // 2
    raw = got_ref[:, PICK:, :].reshape(H * half, PAIR).astype(F32)
    head = jnp.where(low, raw, 0.0)
    tail = jnp.where(low, pltpu.roll(raw, HD, 1), 0.0).reshape(H, half, PAIR)
    tail_two = tail[:, : LOCAL2 - half].reshape(-1, PAIR)
    tail_three = tail[:, LOCAL2 - half :].reshape(-1, PAIR)

    def attend(q, sets):
        q = q.astype(BF16)
        scores = []
        for kv, masked in sets:
            part = lax.dot_general(q, kv, NT, preferred_element_type=F32)
            if masked:
                part = jnp.where(iota((1, kv.shape[0]), 1) % PICK < LOCAL2, part, -1e30)
            scores.append(part)
        largest = functools.reduce(jnp.maximum, [jnp.max(part, axis=-1, keepdims=True) for part in scores])
        total = None
        for (kv, _), part in zip(sets, scores):
            expo = jnp.exp2((part - largest) * SCALE2).astype(BF16)
            part = jnp.dot(expo, jnp.where(low, one, kv), preferred_element_type=F32)
            total = part if total is None else total + part
        weight = total[:, :1]
        log_sum = largest * SCALE2 + jnp.log2(weight)
        top = log_sum.astype(BF16).astype(F32)
        middle = (log_sum - top).astype(BF16).astype(F32)
        rest = log_sum - top - middle
        lane = iota((1, PAIR), 1)
        stats = jnp.where(lane < 16, top, jnp.where(lane < 32, middle, rest))
        return jnp.where(low, stats, total / weight)

    two = ((own, True), (other, True))
    rows = H * half // 2
    first = jnp.concatenate([attend(head[:rows], two), attend(head[rows:], two)], 0)
    first = first.reshape(GRP, XS, half, PAIR)
    second = attend(tail_two, two).reshape(GRP, XS, LOCAL2 - half, PAIR)
    third = attend(tail_three, ((far, False),)).reshape(GRP, XS, PICK - LOCAL2, PAIR)
    second = jnp.concatenate([second, third], axis=2)
    for x in range(XS):
        where = (x - place_ref[0] + XS) % XS
        out_ref[where, :, :half, :] = first[:, x].astype(BF16)
        out_ref[where, :, half:, :] = second[:, x].astype(BF16)


def sparse_levels(place, got, other, far):
    shape = (XS, GRP, PICK, PAIR)
    return pl.pallas_call(
        sparse_kernel,
        in_specs=[pl.BlockSpec(memory_space=pltpu.SMEM)] + [pl.BlockSpec(memory_space=pltpu.VMEM)] * 3,
        out_shape=jax.ShapeDtypeStruct(shape, BF16),
        compiler_params=params(),
        cost_estimate=cost(4 * 10**9, 2 * 10**6, 2 * 10**6),
        name="sparse_levels",
    )(place, got, other, far)


def dense_kernel(head, scalar_ref, q_ref, bulk_ref, back_ref, out_ref, acc, top, aug, few):
    zero, one = jnp.zeros((), BF16), jnp.ones((), BF16)
    keys = slice(PAIR + head * HD, PAIR + head * HD + PAIR)
    values = slice(keys.start + WIDTH, keys.stop + WIDTH)

    def mine(parity, rows):
        lane = iota((rows, PAIR), 1)
        return (lane >= HD) if parity else (lane < HD)

    for parity in range(2):
        aug[parity] = jnp.where(mine(parity, SEG1), bulk_ref[:, values], one)

    def level_one(block, carry):
        rows = pl.ds(pl.multiple_of(block * BLOCK, BLOCK), BLOCK)
        q = q_ref[rows, :PAIR]
        scores = [
            lax.dot_general(jnp.where(mine(parity, BLOCK), q, zero), bulk_ref[:, keys], NT, preferred_element_type=F32)
            for parity in range(2)
        ]
        for parity in range(2):
            largest = jnp.max(scores[parity], axis=-1, keepdims=True)
            expo = jnp.exp2((scores[parity] - largest) * SCALE2).astype(BF16)
            acc[parity, rows, :] = jnp.dot(expo, aug[parity], preferred_element_type=F32)
            top[parity, rows, :] = jnp.broadcast_to(largest * SCALE2, (BLOCK, PAIR))
        return carry

    lax.fori_loop(0, SEG1 // BLOCK, level_one, 0)

    for parity in range(2):
        back = back_ref[(scalar_ref[0] - head - parity + XS) % XS].astype(F32)

        def merge(rows, part, parity=parity):
            log_sum = part[:, 0:1] + part[:, 16:17] + part[:, 32:33]
            shaped = part if parity else pltpu.roll(part, HD, 1)
            shaped = jnp.where(mine(parity, part.shape[0]), shaped, 1.0)
            old = top[parity, rows, :]
            peak = jnp.maximum(old, log_sum)
            top[parity, rows, :] = peak
            acc[parity, rows, :] = acc[parity, rows, :] * jnp.exp2(old - peak) + shaped * jnp.exp2(log_sum - peak)

        two = scalar_ref[1 + parity]
        merge(pl.ds(two, SEG1 // R2, stride=R2), back[:, :LOCAL2].reshape(SEG1 // R2, PAIR))
        for g in range(GRP):
            few[g * LOCAL3 : (g + 1) * LOCAL3, :] = back[g, LOCAL2 : LOCAL2 + LOCAL3]
        three = scalar_ref[3 + parity]
        merge(pl.ds(three, SEG1 // R3, stride=R3), few[...])
    result = [acc[parity] / pltpu.roll(acc[parity], HD, 1) for parity in range(2)]
    out_ref[...] = jnp.where(mine(0, SEG1), result[0], result[1]).astype(BF16)


def dense_level(head, scalars, q, bulk, back):
    return pl.pallas_call(
        functools.partial(dense_kernel, head),
        in_specs=[pl.BlockSpec(memory_space=pltpu.SMEM)] + [pl.BlockSpec(memory_space=pltpu.VMEM)] * 3,
        out_shape=jax.ShapeDtypeStruct((SEG1, PAIR), BF16),
        scratch_shapes=[
            pltpu.VMEM((2, SEG1, PAIR), F32),
            pltpu.VMEM((2, SEG1, PAIR), F32),
            pltpu.VMEM((2, SEG1, PAIR), BF16),
            pltpu.VMEM((SEG1 // R3, PAIR), F32),
        ],
        compiler_params=params(),
        cost_estimate=cost(10 * 10**9, 4 * 10**6, 5 * 10**6),
        name="dense_level",
    )(scalars, q, bulk, back)


def project_kernel(place_ref, first_ref, second_ref, own_ref, other_ref, out_ref):
    part = D // H // 2
    _, zh, x = (place_ref[i] for i in range(3))

    def write(w_ref):
        total = None
        for g in range(GRP):
            weights = []
            for other_zh in range(2):
                for other_x in range(XS):
                    turn = (x - other_x + XS) % XS * 2 + (zh + other_zh) % 2
                    weights.append(w_ref[pl.ds(pl.multiple_of(g * WIDTH + turn * part, part), part), :])
            att = jnp.concatenate([first_ref[g], second_ref[g]], axis=1)
            term = jnp.dot(att, jnp.concatenate(weights, 0), preferred_element_type=F32)
            total = term if total is None else total + term
        out_ref[...] = total.astype(BF16)

    is_own = pl.program_id(0) < pl.num_programs(0) // 2
    pl.when(is_own)(lambda: write(own_ref))
    pl.when(jnp.logical_not(is_own))(lambda: write(other_ref))


def project(place, first, second, own, other):
    columns = 512
    half = D // 2 // columns
    att = pl.BlockSpec((GRP, ROWS, PAIR), lambda j, place: (0, 0, 0))
    return pl.pallas_call(
        project_kernel,
        grid_spec=pltpu.PrefetchScalarGridSpec(
            num_scalar_prefetch=1,
            grid=(2 * half,),
            in_specs=[
                att,
                att,
                pl.BlockSpec((D, columns), lambda j, place: (0, jnp.minimum(j, half - 1))),
                pl.BlockSpec((D, columns), lambda j, place: (0, jnp.maximum(j - half, 0))),
            ],
            out_specs=pl.BlockSpec((ROWS, columns), lambda j, place: (0, (j + place[0] * half) % (2 * half))),
        ),
        out_shape=jax.ShapeDtypeStruct((ROWS, D), BF16),
        compiler_params=pltpu.CompilerParams(vmem_limit_bytes=56 * 2**20),
        cost_estimate=cost(2 * ROWS * D * D, 10 * 10**6),
        name="project",
    )(place, first, second, own, other)


def shift(value, axis, step):
    size = lax.axis_size(axis)
    return lax.ppermute(value, axis, [(i, (i + step) % size) for i in range(size)])


def turns(value, axis):
    return [value] + [shift(value, axis, step) for step in range(1, lax.axis_size(axis))]


def after(value, *events):
    return lax.optimization_barrier((value, *events))[0]


def local(queries, keys, values, offsets_two, offsets_three, w_out):
    half = D // 2
    exchange = functools.partial(lax.all_to_all, axis_name=GROUP, split_axis=0, concat_axis=0, tiled=True)
    x = lax.axis_index("x")
    first_head = lax.axis_index(GROUP) * OWN
    own_two = lax.dynamic_slice_in_dim(offsets_two, first_head, OWN)
    own_three = lax.dynamic_slice_in_dim(offsets_three, first_head, OWN)

    place = jnp.stack([lax.axis_index(name).astype(jnp.int32) for name in ("core", "zh", "x")])

    bulk, rest, small = pack(offsets_two, offsets_three, queries, keys, values)
    got = lax.all_to_all(small, ("zl", "core", "x"), split_axis=0, concat_axis=0, tiled=True)
    bulk = exchange(after(bulk, got)).reshape(SEG1, BULK)
    own = got[:, :PICK]
    other = shift(own, "zh", 1)
    w_rows = lax.dynamic_slice_in_dim(w_out, lax.axis_index("core") * half, half, axis=1)
    w_rows = jnp.concatenate(turns(jnp.concatenate(turns(after(w_rows, got), "zh"), 0), "x"), 0)
    w_own = lax.all_gather(w_rows, "y", axis=0, tiled=True)
    far = lax.all_gather(compact(own.reshape(H * PICK, PAIR), other.reshape(H * PICK, PAIR)), "y", axis=0, tiled=True)
    parts = sparse_levels(x.reshape(1), got, other, far)
    back = jnp.stack([parts[0]] + [shift(parts[step], "x", step) for step in range(1, XS)])
    rest = exchange(after(rest, bulk, back)).reshape(SEG1, PAIR)

    def scalars(head):
        return jnp.concatenate([x.reshape(1), own_two[head : head + 2], own_three[head : head + 2]])

    att_a = dense_level(0, scalars(0), bulk, bulk, back)
    att_b = dense_level(2, scalars(2), rest, bulk, back)
    w_own = after(w_own, att_a)
    w_other = shift(w_own, "core", 1)
    out_a = exchange(att_a.reshape(GRP, ROWS, PAIR))
    out_b = exchange(att_b.reshape(GRP, ROWS, PAIR))
    return project(place, out_a, out_b, w_own, w_other)


def solution(mesh):
    rows = P(("y", "zh", "x", "zl", "core"), None)
    return jax.shard_map(
        local,
        mesh=fine_mesh(mesh),
        in_specs=(rows, rows, rows, P(), P(), P(("y", "zh", "x"), None)),
        out_specs=rows,
        check_vma=False,
    )
```

```python
import functools
import math

import jax
import jax.numpy as jnp
from jax import lax
from jax.experimental import pallas as pl
from jax.experimental.pallas import tpu as pltpu
from jax.sharding import Mesh
from jax.sharding import PartitionSpec as P

H = 32
HD = 64
PAIR = 2 * HD
R2 = 8
R3 = 64
D = H * HD
GRP = 8
XS = 4
ZH = 2
ROWS = 192
SEG1 = ROWS * GRP
OWN = H // GRP
WIDTH = OWN * HD
LOCAL2 = ROWS // R2
LOCAL3 = ROWS // R3
PICK = 32
SENT = PICK + PICK // 2
BLOCK = 256
PART = 256
PER_STEP = 2
SCALE2 = HD**-0.5 * math.log2(math.e)
VMEM_LIMIT = 40 * 2**20
GROUP = ("zl", "core")
NT = (((1,), (1,)), ((), ()))
BF16 = jnp.bfloat16
F32 = jnp.float32


def fine_mesh(mesh):
    return Mesh(mesh.devices.reshape(4, 2, 8, 2, XS), ("zl", "core", "y", "zh", "x"))


def params():
    return pltpu.CompilerParams(vmem_limit_bytes=VMEM_LIMIT)


def cost(flops, traffic, transcendentals=0):
    return pl.CostEstimate(flops=flops, bytes_accessed=traffic, transcendentals=transcendentals)


def iota(shape, dim):
    return lax.broadcasted_iota(jnp.int32, shape, dim)


def pick_kernel(two_ref, three_ref, q_ref, k_ref, v_ref, small_ref):
    for group in range(PER_STEP):
        pick_group(group, two_ref, three_ref, q_ref, k_ref, v_ref, small_ref)


def pick_group(group, two_ref, three_ref, q_ref, k_ref, v_ref, small_ref):
    step = pl.program_id(0) * PER_STEP + group
    columns = slice(group * WIDTH, (group + 1) * WIDTH)
    row = iota((OWN * PICK, ROWS), 0)
    place = row % PICK
    target = jnp.full((OWN * PICK, ROWS), -1, jnp.int32)
    for i in range(OWN):
        two = place * R2 + two_ref[step * OWN + i]
        three = (place - LOCAL2) * R3 + three_ref[step * OWN + i]
        own = jnp.where(place < LOCAL2, two, jnp.where(place < LOCAL2 + LOCAL3, three, -1))
        target = jnp.where(row // PICK == i, own, target)
    onehot = jnp.where(iota((OWN * PICK, ROWS), 1) == target, 1.0, 0.0).astype(BF16)
    picked = [jnp.dot(onehot, ref[:, columns], preferred_element_type=F32) for ref in (q_ref, k_ref, v_ref)]
    low = iota((PICK, PAIR), 1) < HD
    for i in range(OWN):
        rows, lanes = slice(i * PICK, (i + 1) * PICK), slice(i // 2 * PAIR, (i // 2 + 1) * PAIR)
        q, k, v = (part[rows, lanes] for part in picked)
        if i % 2:
            k = pltpu.roll(k, HD, 1)
            head, tail = pltpu.roll(q[: PICK // 2], HD, 1), q[PICK // 2 :]
        else:
            v = pltpu.roll(v, HD, 1)
            head, tail = q[: PICK // 2], pltpu.roll(q[PICK // 2 :], HD, 1)
        kv = jnp.where(low, k, v).astype(BF16)
        lines = jnp.where(low[: PICK // 2], head, tail).astype(BF16)
        for zh in range(ZH):
            small_ref[group * OWN + i, zh, :PICK, :] = kv
            small_ref[group * OWN + i, zh, PICK:, :] = lines


def pick(offsets_two, offsets_three, queries, keys, values):
    block = pl.BlockSpec((ROWS, PER_STEP * WIDTH), lambda j, *_: (0, j))
    return pl.pallas_call(
        pick_kernel,
        grid_spec=pltpu.PrefetchScalarGridSpec(
            num_scalar_prefetch=2,
            grid=(GRP // PER_STEP,),
            in_specs=[block] * 3,
            out_specs=pl.BlockSpec((PER_STEP * OWN, ZH, SENT, PAIR), lambda j, *_: (j, 0, 0, 0)),
        ),
        out_shape=jax.ShapeDtypeStruct((H, ZH, SENT, PAIR), BF16),
        compiler_params=pltpu.CompilerParams(vmem_limit_bytes=56 * 2**20),
        cost_estimate=cost(10**9, 4 * 10**6),
        name="pick",
    )(offsets_two, offsets_three, queries, keys, values)


def pack_kernel(q_ref, k_ref, v_ref, first_ref, second_ref):
    for pair, out_ref in enumerate((first_ref, second_ref)):
        for which, ref in enumerate((q_ref, k_ref, v_ref)):
            out_ref[0, :, which * PAIR : (which + 1) * PAIR] = ref[:, pair * PAIR : (pair + 1) * PAIR]


def pack(queries, keys, values):
    block = pl.BlockSpec((ROWS, WIDTH), lambda j: (0, j))
    chunk = pl.BlockSpec((1, ROWS, 3 * PAIR), lambda j: (j, 0, 0))
    shape = jax.ShapeDtypeStruct((GRP, ROWS, 3 * PAIR), BF16)
    return pl.pallas_call(
        pack_kernel,
        grid=(GRP,),
        in_specs=[block] * 3,
        out_specs=[chunk] * 2,
        out_shape=[shape] * 2,
        compiler_params=pltpu.CompilerParams(vmem_limit_bytes=56 * 2**20),
        cost_estimate=cost(0, 5 * 10**6),
        name="pack",
    )(queries, keys, values)


def compact_kernel(got_ref, out_ref):
    count, keys = ZH * H * LOCAL3, ZH * H * PICK
    row = iota((count, keys), 0)
    target = row // LOCAL3 * PICK + LOCAL2 + row % LOCAL3
    onehot = jnp.where(iota((count, keys), 1) == target, 1.0, 0.0).astype(BF16)
    chosen = jnp.dot(onehot, got_ref[:, :, :PICK, :].reshape(keys, PAIR), preferred_element_type=F32)
    out_ref[...] = chosen.astype(BF16)


def compact(got):
    return pl.pallas_call(
        compact_kernel,
        out_shape=jax.ShapeDtypeStruct((ZH * H * LOCAL3, PAIR), BF16),
        compiler_params=params(),
        cost_estimate=cost(10**8, 10**6),
        name="compact_three",
    )(got)


def sparse_kernel(place_ref, got_ref, far_ref, out_ref):
    low = iota((1, PAIR), 1) < HD
    one = jnp.ones((), BF16)
    near = got_ref[:, :, :PICK, :].reshape(ZH * H * PICK, PAIR)
    far = far_ref[...]
    half = PICK // 2
    raw = got_ref[:, pl.ds(place_ref[1], 1), PICK:, :].reshape(H * half, PAIR).astype(F32)
    head = jnp.where(low, raw, 0.0)
    tail = jnp.where(low, pltpu.roll(raw, HD, 1), 0.0).reshape(H, half, PAIR)
    tail_two = tail[:, : LOCAL2 - half].reshape(-1, PAIR)
    tail_three = tail[:, LOCAL2 - half :].reshape(-1, PAIR)

    def attend(q, kv, masked):
        scores = lax.dot_general(q.astype(BF16), kv, NT, preferred_element_type=F32)
        if masked:
            scores = jnp.where(iota((1, kv.shape[0]), 1) % PICK < LOCAL2, scores, -1e30)
        largest = jnp.max(scores, axis=-1, keepdims=True)
        expo = jnp.exp2((scores - largest) * SCALE2).astype(BF16)
        total = jnp.dot(expo, jnp.where(low, one, kv), preferred_element_type=F32)
        weight = total[:, :1]
        log_sum = largest * SCALE2 + jnp.log2(weight)
        top = log_sum.astype(BF16).astype(F32)
        middle = (log_sum - top).astype(BF16).astype(F32)
        rest = log_sum - top - middle
        lane = iota((1, PAIR), 1)
        stats = jnp.where(lane < 16, top, jnp.where(lane < 32, middle, rest))
        return jnp.where(low, stats, total / weight)

    rows = H * half // 2
    first = jnp.concatenate([attend(head[:rows], near, True), attend(head[rows:], near, True)], 0)
    first = first.reshape(GRP, XS, half, PAIR)
    second = attend(tail_two, near, True).reshape(GRP, XS, LOCAL2 - half, PAIR)
    third = attend(tail_three, far, False).reshape(GRP, XS, PICK - LOCAL2, PAIR)
    second = jnp.concatenate([second, third], axis=2)
    for x in range(XS):
        where = (x - place_ref[0] + XS) % XS
        out_ref[where, :, :half, :] = first[:, x].astype(BF16)
        out_ref[where, :, half:, :] = second[:, x].astype(BF16)


def sparse_levels(place, got, far):
    shape = (XS, GRP, PICK, PAIR)
    return pl.pallas_call(
        sparse_kernel,
        in_specs=[pl.BlockSpec(memory_space=pltpu.SMEM)] + [pl.BlockSpec(memory_space=pltpu.VMEM)] * 2,
        out_shape=jax.ShapeDtypeStruct(shape, BF16),
        compiler_params=params(),
        cost_estimate=cost(4 * 10**9, 2 * 10**6, 2 * 10**6),
        name="sparse_levels",
    )(place, got, far)


def dense_kernel(pair, scalar_ref, qkv_ref, back_ref, out_ref, acc, top, aug, scores, few):
    zero, one = jnp.zeros((), BF16), jnp.ones((), BF16)
    blocks, parts = SEG1 // BLOCK, SEG1 // PART

    def mine(parity, rows):
        lane = iota((rows, PAIR), 1)
        return (lane >= HD) if parity else (lane < HD)

    def rows_of(block):
        return pl.ds(pl.multiple_of(block * BLOCK, BLOCK), BLOCK)

    columns, keys, values = (slice(i * PAIR, (i + 1) * PAIR) for i in range(3))
    for parity in range(2):
        aug[parity] = jnp.where(mine(parity, SEG1), qkv_ref[:, values], one)

    def step(ahead, parity, largest, block):
        q, expected, total = None, None, None
        if ahead is not None:
            q = jnp.where(mine(ahead[0], BLOCK), qkv_ref[rows_of(ahead[1]), columns], zero)
        for part in range(parts):
            lanes = slice(part * PART, (part + 1) * PART)
            if ahead is not None:
                fresh = lax.dot_general(q, qkv_ref[lanes, keys], NT, preferred_element_type=F32)
                scores[ahead[0], :, lanes] = fresh
                for i in range(0, PART, PAIR):
                    piece = fresh[:, i : i + PAIR]
                    expected = piece if expected is None else jnp.maximum(expected, piece)
            if parity is not None:
                expo = jnp.exp2((scores[parity, :, lanes] - largest) * SCALE2).astype(BF16)
                term = jnp.dot(expo, aug[parity, lanes, :], preferred_element_type=F32)
                total = term if total is None else total + term
        if parity is not None:
            acc[parity, rows_of(block), :] = total
            top[parity, rows_of(block), :] = jnp.broadcast_to(largest * SCALE2, (BLOCK, PAIR))
        if ahead is not None:
            return jnp.max(expected, axis=-1, keepdims=True)

    def level_one(block, largest):
        other = step((1, block), 0, largest, block)
        return step((0, jnp.minimum(block + 1, blocks - 1)), 1, other, block)

    lax.fori_loop(0, blocks, level_one, step((0, 0), None, None, None))

    for parity in range(2):
        head = pair * 2 + parity
        back = back_ref[(scalar_ref[0] - head + XS) % XS].astype(F32)

        def merge(rows, part, parity=parity):
            log_sum = part[:, 0:1] + part[:, 16:17] + part[:, 32:33]
            shaped = part if parity else pltpu.roll(part, HD, 1)
            shaped = jnp.where(mine(parity, part.shape[0]), shaped, 1.0)
            old = top[parity, rows, :]
            peak = jnp.maximum(old, log_sum)
            top[parity, rows, :] = peak
            acc[parity, rows, :] = acc[parity, rows, :] * jnp.exp2(old - peak) + shaped * jnp.exp2(log_sum - peak)

        merge(pl.ds(scalar_ref[1 + head], SEG1 // R2, stride=R2), back[:, :LOCAL2].reshape(SEG1 // R2, PAIR))
        for g in range(GRP):
            few[g * LOCAL3 : (g + 1) * LOCAL3, :] = back[g, LOCAL2 : LOCAL2 + LOCAL3]
        merge(pl.ds(scalar_ref[1 + OWN + head], SEG1 // R3, stride=R3), few[...])
    result = [acc[parity] / pltpu.roll(acc[parity], HD, 1) for parity in range(2)]
    out_ref[...] = jnp.where(mine(0, SEG1), result[0], result[1]).astype(BF16)


def dense_level(pair, scalars, qkv, back):
    return pl.pallas_call(
        functools.partial(dense_kernel, pair),
        in_specs=[pl.BlockSpec(memory_space=pltpu.SMEM)] + [pl.BlockSpec(memory_space=pltpu.VMEM)] * 2,
        out_shape=jax.ShapeDtypeStruct((SEG1, PAIR), BF16),
        scratch_shapes=[
            pltpu.VMEM((2, SEG1, PAIR), F32),
            pltpu.VMEM((2, SEG1, PAIR), F32),
            pltpu.VMEM((2, SEG1, PAIR), BF16),
            pltpu.VMEM((2, BLOCK, SEG1), F32),
            pltpu.VMEM((SEG1 // R3, PAIR), F32),
        ],
        compiler_params=params(),
        cost_estimate=cost(10 * 10**9, 2 * 10**6, 5 * 10**6),
        name="dense_level",
    )(scalars, qkv, back)


def project_kernel(place_ref, first_ref, second_ref, own_ref, own_far_ref, other_ref, other_far_ref, out_ref):
    upper = place_ref[1] == 1
    part = WIDTH // ZH

    def write(near_ref, far_ref):
        total = None
        for g in range(GRP):
            rows = slice(g * part, (g + 1) * part)
            near = jnp.where(upper, second_ref[g], first_ref[g])
            far = jnp.where(upper, first_ref[g], second_ref[g])
            term = jnp.dot(
                jnp.concatenate([near, far], 1),
                jnp.concatenate([near_ref[rows, :], far_ref[rows, :]], 0),
                preferred_element_type=F32,
            )
            total = term if total is None else total + term
        out_ref[...] = total.astype(BF16)

    is_own = pl.program_id(0) < pl.num_programs(0) // 2
    pl.when(is_own)(lambda: write(own_ref, own_far_ref))
    pl.when(jnp.logical_not(is_own))(lambda: write(other_ref, other_far_ref))


def project(place, first, second, own, own_far, other, other_far):
    columns = 512
    half = D // 2 // columns
    att = pl.BlockSpec((GRP, ROWS, PAIR), lambda j, place: (0, 0, 0))
    early = pl.BlockSpec((D // ZH, columns), lambda j, place: (0, jnp.minimum(j, half - 1)))
    late = pl.BlockSpec((D // ZH, columns), lambda j, place: (0, jnp.maximum(j - half, 0)))
    return pl.pallas_call(
        project_kernel,
        grid_spec=pltpu.PrefetchScalarGridSpec(
            num_scalar_prefetch=1,
            grid=(2 * half,),
            in_specs=[att, att, early, early, late, late],
            out_specs=pl.BlockSpec((ROWS, columns), lambda j, place: (0, (j + place[0] * half) % (2 * half))),
        ),
        out_shape=jax.ShapeDtypeStruct((ROWS, D), BF16),
        compiler_params=pltpu.CompilerParams(vmem_limit_bytes=24 * 2**20),
        cost_estimate=cost(2 * ROWS * D * D, 10 * 10**6),
        name="project",
    )(place, first, second, own, own_far, other, other_far)


def shift(value, axis, step):
    size = lax.axis_size(axis)
    return lax.ppermute(value, axis, [(i, (i + step) % size) for i in range(size)])


def after(value, *events):
    return lax.optimization_barrier((value, *events))[0]


def local(queries, keys, values, offsets_two, offsets_three, w_out):
    half = D // 2
    exchange = functools.partial(lax.all_to_all, axis_name=GROUP, split_axis=0, concat_axis=0, tiled=True)
    x = lax.axis_index("x")
    first_head = lax.axis_index(GROUP) * OWN
    own_two = lax.dynamic_slice_in_dim(offsets_two, first_head, OWN)
    own_three = lax.dynamic_slice_in_dim(offsets_three, first_head, OWN)

    core, zh = lax.axis_index("core"), lax.axis_index("zh")

    w_rows = lax.dynamic_slice_in_dim(w_out, core * half, half, axis=1)
    w_own = lax.all_gather(w_rows, ("y", "x"), axis=0, tiled=True)
    small = pick(offsets_two, offsets_three, queries, keys, values)
    chunk_a, chunk_b = pack(after(queries, small), keys, values)
    got = lax.all_to_all(
        small.reshape(H * ZH, SENT, PAIR), ("zl", "core", "x", "zh"), split_axis=0, concat_axis=0, tiled=True
    ).reshape(H, ZH, SENT, PAIR)
    far_rows = shift(after(w_rows, chunk_a), "zh", 1)
    w_own_far = lax.all_gather(far_rows, ("y", "x"), axis=0, tiled=True)

    qkv_a = exchange(after(chunk_a, got, far_rows)).reshape(SEG1, 3 * PAIR)
    far = lax.all_gather(compact(got), "y", axis=0, tiled=True)
    qkv_b = exchange(after(chunk_b, qkv_a, far)).reshape(SEG1, 3 * PAIR)
    parts = sparse_levels(jnp.stack([x, zh]), got, far)
    back = jnp.stack([parts[0]] + [shift(parts[step], "x", step) for step in range(1, XS)])
    scalars = jnp.concatenate([x.reshape(1), own_two, own_three])
    att_a = dense_level(0, scalars, qkv_a, back)
    out_a = exchange(after(att_a, qkv_b).reshape(GRP, ROWS, PAIR))
    att_b = dense_level(1, scalars, after(qkv_b, att_a), back)
    out_b = exchange(att_b.reshape(GRP, ROWS, PAIR))
    w_other = shift(after(w_own, att_a), "core", 1)
    w_other_far = shift(after(w_own_far, att_b), "core", 1)
    return project(jnp.stack([core, zh]), out_a, out_b, w_own, w_own_far, w_other, w_other_far)


def solution(mesh):
    rows = P(("y", "zh", "x", "zl", "core"), None)
    return jax.shard_map(
        local,
        mesh=fine_mesh(mesh),
        in_specs=(rows, rows, rows, P(), P(), P(("y", "zh", "x"), None)),
        out_specs=rows,
        check_vma=False,
    )
```

```python
import functools
import math

import jax
import jax.numpy as jnp
from jax import lax
from jax.experimental import pallas as pl
from jax.experimental.pallas import tpu as pltpu
from jax.sharding import Mesh
from jax.sharding import PartitionSpec as P

H = 32
HD = 64
PAIR = 2 * HD
R2 = 8
R3 = 64
D = H * HD
GRP = 8
XS = 4
ZH = 2
ROWS = 192
SEG1 = ROWS * GRP
OWN = H // GRP
WIDTH = OWN * HD
LOCAL2 = ROWS // R2
LOCAL3 = ROWS // R3
PICK = 32
SENT = PICK + PICK // 2
BLOCK = 512
PART = 256
BULK = PAIR + 2 * WIDTH
PER_STEP = 2
SCALE2 = HD**-0.5 * math.log2(math.e)
VMEM_LIMIT = 28 * 2**20
GROUP = ("zl", "core")
NT = (((1,), (1,)), ((), ()))
BF16 = jnp.bfloat16
F32 = jnp.float32


def fine_mesh(mesh):
    return Mesh(mesh.devices.reshape(4, 2, 8, 2, XS), ("zl", "core", "y", "zh", "x"))


def params():
    return pltpu.CompilerParams(vmem_limit_bytes=VMEM_LIMIT)


def cost(flops, traffic, transcendentals=0):
    return pl.CostEstimate(flops=flops, bytes_accessed=traffic, transcendentals=transcendentals)


def iota(shape, dim):
    return lax.broadcasted_iota(jnp.int32, shape, dim)


def pick_kernel(two_ref, three_ref, q_ref, k_ref, v_ref, small_ref):
    for group in range(PER_STEP):
        pick_group(group, two_ref, three_ref, q_ref, k_ref, v_ref, small_ref)


def pick_group(group, two_ref, three_ref, q_ref, k_ref, v_ref, small_ref):
    step = pl.program_id(0) * PER_STEP + group
    columns = slice(group * WIDTH, (group + 1) * WIDTH)
    row = iota((OWN * PICK, ROWS), 0)
    place = row % PICK
    target = jnp.full((OWN * PICK, ROWS), -1, jnp.int32)
    for i in range(OWN):
        two = place * R2 + two_ref[step * OWN + i]
        three = (place - LOCAL2) * R3 + three_ref[step * OWN + i]
        own = jnp.where(place < LOCAL2, two, jnp.where(place < LOCAL2 + LOCAL3, three, -1))
        target = jnp.where(row // PICK == i, own, target)
    onehot = jnp.where(iota((OWN * PICK, ROWS), 1) == target, 1.0, 0.0).astype(BF16)
    picked = [jnp.dot(onehot, ref[:, columns], preferred_element_type=F32) for ref in (q_ref, k_ref, v_ref)]
    low = iota((PICK, PAIR), 1) < HD
    for i in range(OWN):
        rows, lanes = slice(i * PICK, (i + 1) * PICK), slice(i // 2 * PAIR, (i // 2 + 1) * PAIR)
        q, k, v = (part[rows, lanes] for part in picked)
        if i % 2:
            k = pltpu.roll(k, HD, 1)
            head, tail = pltpu.roll(q[: PICK // 2], HD, 1), q[PICK // 2 :]
        else:
            v = pltpu.roll(v, HD, 1)
            head, tail = q[: PICK // 2], pltpu.roll(q[PICK // 2 :], HD, 1)
        kv = jnp.where(low, k, v).astype(BF16)
        lines = jnp.where(low[: PICK // 2], head, tail).astype(BF16)
        for zh in range(ZH):
            small_ref[group * OWN + i, zh, :PICK, :] = kv
            small_ref[group * OWN + i, zh, PICK:, :] = lines


def pick(offsets_two, offsets_three, queries, keys, values):
    block = pl.BlockSpec((ROWS, PER_STEP * WIDTH), lambda j, *_: (0, j))
    return pl.pallas_call(
        pick_kernel,
        grid_spec=pltpu.PrefetchScalarGridSpec(
            num_scalar_prefetch=2,
            grid=(GRP // PER_STEP,),
            in_specs=[block] * 3,
            out_specs=pl.BlockSpec((PER_STEP * OWN, ZH, SENT, PAIR), lambda j, *_: (j, 0, 0, 0)),
        ),
        out_shape=jax.ShapeDtypeStruct((H, ZH, SENT, PAIR), BF16),
        compiler_params=pltpu.CompilerParams(vmem_limit_bytes=56 * 2**20),
        cost_estimate=cost(10**9, 4 * 10**6),
        name="pick",
    )(offsets_two, offsets_three, queries, keys, values)


def pack_kernel(q_ref, k_ref, v_ref, bulk_ref, rest_ref):
    bulk_ref[0, :, :PAIR] = q_ref[:, :PAIR]
    bulk_ref[0, :, PAIR : PAIR + WIDTH] = k_ref[...]
    bulk_ref[0, :, PAIR + WIDTH :] = v_ref[...]
    rest_ref[0] = q_ref[:, PAIR:]


def pack(queries, keys, values):
    block = pl.BlockSpec((ROWS, WIDTH), lambda j: (0, j))
    return pl.pallas_call(
        pack_kernel,
        grid=(GRP,),
        in_specs=[block] * 3,
        out_specs=[pl.BlockSpec((1, ROWS, columns), lambda j: (j, 0, 0)) for columns in (BULK, PAIR)],
        out_shape=[jax.ShapeDtypeStruct((GRP, ROWS, columns), BF16) for columns in (BULK, PAIR)],
        compiler_params=pltpu.CompilerParams(vmem_limit_bytes=56 * 2**20),
        cost_estimate=cost(0, 5 * 10**6),
        name="pack",
    )(queries, keys, values)


def compact_kernel(got_ref, out_ref):
    count, keys = ZH * H * LOCAL3, ZH * H * PICK
    row = iota((count, keys), 0)
    target = row // LOCAL3 * PICK + LOCAL2 + row % LOCAL3
    onehot = jnp.where(iota((count, keys), 1) == target, 1.0, 0.0).astype(BF16)
    chosen = jnp.dot(onehot, got_ref[:, :, :PICK, :].reshape(keys, PAIR), preferred_element_type=F32)
    out_ref[...] = chosen.astype(BF16)


def compact(got):
    return pl.pallas_call(
        compact_kernel,
        out_shape=jax.ShapeDtypeStruct((ZH * H * LOCAL3, PAIR), BF16),
        compiler_params=params(),
        cost_estimate=cost(10**8, 10**6),
        name="compact_three",
    )(got)


def sparse_kernel(place_ref, got_ref, far_ref, out_ref):
    low = iota((1, PAIR), 1) < HD
    one = jnp.ones((), BF16)
    near = got_ref[:, :, :PICK, :].reshape(ZH * H * PICK, PAIR)
    far = far_ref[...]
    half = PICK // 2
    raw = got_ref[:, pl.ds(place_ref[1], 1), PICK:, :].reshape(H * half, PAIR).astype(F32)
    head = jnp.where(low, raw, 0.0)
    tail = jnp.where(low, pltpu.roll(raw, HD, 1), 0.0).reshape(H, half, PAIR)
    tail_two = tail[:, : LOCAL2 - half].reshape(-1, PAIR)
    tail_three = tail[:, LOCAL2 - half :].reshape(-1, PAIR)

    def attend(q, kv, masked):
        scores = lax.dot_general(q.astype(BF16), kv, NT, preferred_element_type=F32)
        if masked:
            scores = jnp.where(iota((1, kv.shape[0]), 1) % PICK < LOCAL2, scores, -1e30)
        largest = jnp.max(scores, axis=-1, keepdims=True)
        expo = jnp.exp2((scores - largest) * SCALE2).astype(BF16)
        total = jnp.dot(expo, jnp.where(low, one, kv), preferred_element_type=F32)
        weight = total[:, :1]
        log_sum = largest * SCALE2 + jnp.log2(weight)
        top = log_sum.astype(BF16).astype(F32)
        middle = (log_sum - top).astype(BF16).astype(F32)
        rest = log_sum - top - middle
        lane = iota((1, PAIR), 1)
        stats = jnp.where(lane < 16, top, jnp.where(lane < 32, middle, rest))
        return jnp.where(low, stats, total / weight)

    rows = H * half // 2
    first = jnp.concatenate([attend(head[:rows], near, True), attend(head[rows:], near, True)], 0)
    first = first.reshape(GRP, XS, half, PAIR)
    second = attend(tail_two, near, True).reshape(GRP, XS, LOCAL2 - half, PAIR)
    third = attend(tail_three, far, False).reshape(GRP, XS, PICK - LOCAL2, PAIR)
    second = jnp.concatenate([second, third], axis=2)
    for x in range(XS):
        where = (x - place_ref[0] + XS) % XS
        out_ref[where, :, :half, :] = first[:, x].astype(BF16)
        out_ref[where, :, half:, :] = second[:, x].astype(BF16)


def sparse_levels(place, got, far):
    shape = (XS, GRP, PICK, PAIR)
    return pl.pallas_call(
        sparse_kernel,
        in_specs=[pl.BlockSpec(memory_space=pltpu.SMEM)] + [pl.BlockSpec(memory_space=pltpu.VMEM)] * 2,
        out_shape=jax.ShapeDtypeStruct(shape, BF16),
        compiler_params=params(),
        cost_estimate=cost(4 * 10**9, 2 * 10**6, 2 * 10**6),
        name="sparse_levels",
    )(place, got, far)


def dense_kernel(pair, scalar_ref, q_ref, bulk_ref, back_ref, done_ref, out_ref, acc, top, aug, scores, few):
    zero, one = jnp.zeros((), BF16), jnp.ones((), BF16)
    blocks, parts = SEG1 // BLOCK, SEG1 // PART

    def mine(parity, rows):
        lane = iota((rows, PAIR), 1)
        return (lane >= HD) if parity else (lane < HD)

    def rows_of(block):
        return pl.ds(pl.multiple_of(block * BLOCK, BLOCK), BLOCK)

    keys = slice(PAIR + pair * PAIR, PAIR + (pair + 1) * PAIR)
    values = slice(keys.start + WIDTH, keys.stop + WIDTH)
    for parity in range(2):
        aug[parity] = jnp.where(mine(parity, SEG1), bulk_ref[:, values], one)

    def step(ahead, parity, largest, block):
        q, expected, total = None, None, None
        if ahead is not None:
            q = jnp.where(mine(ahead[0], BLOCK), q_ref[rows_of(ahead[1]), :PAIR], zero)
        for part in range(parts):
            lanes = slice(part * PART, (part + 1) * PART)
            if ahead is not None:
                fresh = lax.dot_general(q, bulk_ref[lanes, keys], NT, preferred_element_type=F32)
                scores[ahead[0], :, lanes] = fresh
                for i in range(0, PART, PAIR):
                    piece = fresh[:, i : i + PAIR]
                    expected = piece if expected is None else jnp.maximum(expected, piece)
            if parity is not None:
                expo = jnp.exp2((scores[parity, :, lanes] - largest) * SCALE2).astype(BF16)
                term = jnp.dot(expo, aug[parity, lanes, :], preferred_element_type=F32)
                total = term if total is None else total + term
        if parity is not None:
            acc[parity, rows_of(block), :] = total
            top[parity, rows_of(block), :] = jnp.broadcast_to(largest * SCALE2, (BLOCK, PAIR))
        if ahead is not None:
            return jnp.max(expected, axis=-1, keepdims=True)

    def level_one(block, largest):
        other = step((1, block), 0, largest, block)
        return step((0, jnp.minimum(block + 1, blocks - 1)), 1, other, block)

    lax.fori_loop(0, blocks, level_one, step((0, 0), None, None, None))

    for parity in range(2):
        head = pair * 2 + parity
        back = back_ref[(scalar_ref[0] - head + XS) % XS].astype(F32)

        def merge(rows, part, parity=parity):
            log_sum = part[:, 0:1] + part[:, 16:17] + part[:, 32:33]
            shaped = part if parity else pltpu.roll(part, HD, 1)
            shaped = jnp.where(mine(parity, part.shape[0]), shaped, 1.0)
            old = top[parity, rows, :]
            peak = jnp.maximum(old, log_sum)
            top[parity, rows, :] = peak
            acc[parity, rows, :] = acc[parity, rows, :] * jnp.exp2(old - peak) + shaped * jnp.exp2(log_sum - peak)

        merge(pl.ds(scalar_ref[1 + head], SEG1 // R2, stride=R2), back[:, :LOCAL2].reshape(SEG1 // R2, PAIR))
        for g in range(GRP):
            few[g * LOCAL3 : (g + 1) * LOCAL3, :] = back[g, LOCAL2 : LOCAL2 + LOCAL3]
        merge(pl.ds(scalar_ref[1 + OWN + head], SEG1 // R3, stride=R3), few[...])
    result = [acc[parity] / pltpu.roll(acc[parity], HD, 1) for parity in range(2)]
    result = jnp.where(mine(0, SEG1), result[0], result[1]).astype(BF16)
    if pair:
        out_ref[:, :PAIR] = done_ref[...]
        out_ref[:, PAIR:] = result
    else:
        out_ref[...] = result


def dense_level(pair, scalars, q, bulk, back, done):
    return pl.pallas_call(
        functools.partial(dense_kernel, pair),
        in_specs=[pl.BlockSpec(memory_space=pltpu.SMEM)] + [pl.BlockSpec(memory_space=pltpu.VMEM)] * 4,
        out_shape=jax.ShapeDtypeStruct((SEG1, PAIR * (pair + 1)), BF16),
        scratch_shapes=[
            pltpu.VMEM((2, SEG1, PAIR), F32),
            pltpu.VMEM((2, SEG1, PAIR), F32),
            pltpu.VMEM((2, SEG1, PAIR), BF16),
            pltpu.VMEM((2, BLOCK, SEG1), F32),
            pltpu.VMEM((SEG1 // R3, PAIR), F32),
        ],
        compiler_params=params(),
        cost_estimate=cost(10 * 10**9, 2 * 10**6, 5 * 10**6),
        name="dense_level",
    )(scalars, q, bulk, back, done)


def project_kernel(place_ref, att_ref, own_ref, other_ref, out_ref):
    upper = place_ref[1] == 1
    part = WIDTH // (XS * ZH)

    def write(w_ref):
        total = None
        for g in range(GRP):
            starts = [g * WIDTH + (x * ZH + far) * part for far in range(ZH) for x in range(XS)]
            weights = jnp.concatenate([w_ref[start : start + part, :] for start in starts], 0)
            low, high = att_ref[g, :, :PAIR], att_ref[g, :, PAIR:]
            att = jnp.concatenate([jnp.where(upper, high, low), jnp.where(upper, low, high)], 1)
            term = jnp.dot(att, weights, preferred_element_type=F32)
            total = term if total is None else total + term
        out_ref[...] = total.astype(BF16)

    is_own = pl.program_id(0) < pl.num_programs(0) // 2
    pl.when(is_own)(lambda: write(own_ref))
    pl.when(jnp.logical_not(is_own))(lambda: write(other_ref))


def project(place, att, own, other):
    columns = 256
    half = D // 2 // columns
    return pl.pallas_call(
        project_kernel,
        grid_spec=pltpu.PrefetchScalarGridSpec(
            num_scalar_prefetch=1,
            grid=(2 * half,),
            in_specs=[
                pl.BlockSpec((GRP, ROWS, WIDTH), lambda j, place: (0, 0, 0)),
                pl.BlockSpec((D, columns), lambda j, place: (0, jnp.minimum(j, half - 1))),
                pl.BlockSpec((D, columns), lambda j, place: (0, jnp.maximum(j - half, 0))),
            ],
            out_specs=pl.BlockSpec((ROWS, columns), lambda j, place: (0, (j + place[0] * half) % (2 * half))),
        ),
        out_shape=jax.ShapeDtypeStruct((ROWS, D), BF16),
        compiler_params=pltpu.CompilerParams(vmem_limit_bytes=24 * 2**20),
        cost_estimate=cost(2 * ROWS * D * D, 10 * 10**6),
        name="project",
    )(place, att, own, other)


def shift(value, axis, step):
    size = lax.axis_size(axis)
    return lax.ppermute(value, axis, [(i, (i + step) % size) for i in range(size)])


def after(value, *events):
    return lax.optimization_barrier((value, *events))[0]


def local(queries, keys, values, offsets_two, offsets_three, w_out):
    half = D // 2
    exchange = functools.partial(lax.all_to_all, axis_name=GROUP, split_axis=0, concat_axis=0, tiled=True)
    x = lax.axis_index("x")
    first_head = lax.axis_index(GROUP) * OWN
    own_two = lax.dynamic_slice_in_dim(offsets_two, first_head, OWN)
    own_three = lax.dynamic_slice_in_dim(offsets_three, first_head, OWN)

    core, zh = lax.axis_index("core"), lax.axis_index("zh")

    w_rows = lax.dynamic_slice_in_dim(w_out, core * half, half, axis=1)
    far_rows = shift(w_rows, "zh", 1)
    small = pick(offsets_two, offsets_three, queries, keys, values)
    bulk, rest = pack(after(queries, small), keys, values)
    w_rows = jnp.concatenate([after(w_rows, small), far_rows], 0)
    w_own = lax.all_gather(w_rows, ("y", "x"), axis=0, tiled=True)
    got = lax.all_to_all(
        after(small, far_rows).reshape(H * ZH, SENT, PAIR), ("zl", "core", "x", "zh"), split_axis=0, concat_axis=0, tiled=True
    ).reshape(H, ZH, SENT, PAIR)

    bulk = exchange(after(bulk, got)).reshape(SEG1, BULK)
    far = lax.all_gather(compact(got), "y", axis=0, tiled=True)
    parts = sparse_levels(jnp.stack([x, zh]), got, far)
    back = jnp.stack([parts[0]] + [shift(parts[step], "x", step) for step in range(1, XS)])
    rest = exchange(after(rest, bulk, back)).reshape(SEG1, PAIR)
    scalars = jnp.concatenate([x.reshape(1), own_two, own_three])
    att = dense_level(0, scalars, bulk, bulk, back, back)
    att = dense_level(1, scalars, rest, bulk, back, att)
    w_other = shift(after(w_own, att), "core", 1)
    att = exchange(att.reshape(GRP, ROWS, WIDTH))
    return project(jnp.stack([core, zh]), att, w_own, w_other)


def solution(mesh):
    rows = P(("y", "zh", "x", "zl", "core"), None)
    return jax.shard_map(
        local,
        mesh=fine_mesh(mesh),
        in_specs=(rows, rows, rows, P(), P(), P(("y", "zh", "x"), None)),
        out_specs=rows,
        check_vma=False,
    )
```

```python
import functools
import math

import jax
import jax.numpy as jnp
from jax import lax
from jax.experimental import pallas as pl
from jax.experimental.pallas import tpu as pltpu
from jax.sharding import Mesh
from jax.sharding import PartitionSpec as P

H = 32
HD = 64
PAIR = 2 * HD
R2 = 8
R3 = 64
D = H * HD
GRP = 8
XS = 4
ZH = 2
ROWS = 192
SEG1 = ROWS * GRP
OWN = H // GRP
WIDTH = OWN * HD
LOCAL2 = ROWS // R2
LOCAL3 = ROWS // R3
PICK = 32
SENT = PICK + PICK // 2
BLOCK = 512
PART = 256
BULK = PAIR + 2 * WIDTH
PER_STEP = 4
SCALE2 = HD**-0.5 * math.log2(math.e)
VMEM_LIMIT = 28 * 2**20
GROUP = ("zl", "core")
NT = (((1,), (1,)), ((), ()))
BF16 = jnp.bfloat16
F32 = jnp.float32


def fine_mesh(mesh):
    return Mesh(mesh.devices.reshape(4, 2, 8, 2, XS), ("zl", "core", "y", "zh", "x"))


def params():
    return pltpu.CompilerParams(vmem_limit_bytes=VMEM_LIMIT)


def cost(flops, traffic, transcendentals=0):
    return pl.CostEstimate(flops=flops, bytes_accessed=traffic, transcendentals=transcendentals)


def iota(shape, dim):
    return lax.broadcasted_iota(jnp.int32, shape, dim)


def pick_kernel(two_ref, three_ref, q_ref, k_ref, v_ref, small_ref):
    for group in range(PER_STEP):
        pick_group(group, two_ref, three_ref, q_ref, k_ref, v_ref, small_ref)


def pick_group(group, two_ref, three_ref, q_ref, k_ref, v_ref, small_ref):
    step = pl.program_id(0) * PER_STEP + group
    columns = slice(group * WIDTH, (group + 1) * WIDTH)
    row = iota((OWN * PICK, ROWS), 0)
    place = row % PICK
    target = jnp.full((OWN * PICK, ROWS), -1, jnp.int32)
    for i in range(OWN):
        two = place * R2 + two_ref[step * OWN + i]
        three = (place - LOCAL2) * R3 + three_ref[step * OWN + i]
        own = jnp.where(place < LOCAL2, two, jnp.where(place < LOCAL2 + LOCAL3, three, -1))
        target = jnp.where(row // PICK == i, own, target)
    onehot = jnp.where(iota((OWN * PICK, ROWS), 1) == target, 1.0, 0.0).astype(BF16)
    picked = [jnp.dot(onehot, ref[:, columns], preferred_element_type=F32) for ref in (q_ref, k_ref, v_ref)]
    low = iota((PICK, PAIR), 1) < HD
    for i in range(OWN):
        rows, lanes = slice(i * PICK, (i + 1) * PICK), slice(i // 2 * PAIR, (i // 2 + 1) * PAIR)
        q, k, v = (part[rows, lanes] for part in picked)
        if i % 2:
            k = pltpu.roll(k, HD, 1)
            head, tail = pltpu.roll(q[: PICK // 2], HD, 1), q[PICK // 2 :]
        else:
            v = pltpu.roll(v, HD, 1)
            head, tail = q[: PICK // 2], pltpu.roll(q[PICK // 2 :], HD, 1)
        kv = jnp.where(low, k, v).astype(BF16)
        lines = jnp.where(low[: PICK // 2], head, tail).astype(BF16)
        for zh in range(ZH):
            small_ref[group * OWN + i, zh, :PICK, :] = kv
            small_ref[group * OWN + i, zh, PICK:, :] = lines


def pick(offsets_two, offsets_three, queries, keys, values):
    block = pl.BlockSpec((ROWS, PER_STEP * WIDTH), lambda j, *_: (0, j))
    return pl.pallas_call(
        pick_kernel,
        grid_spec=pltpu.PrefetchScalarGridSpec(
            num_scalar_prefetch=2,
            grid=(GRP // PER_STEP,),
            in_specs=[block] * 3,
            out_specs=pl.BlockSpec((PER_STEP * OWN, ZH, SENT, PAIR), lambda j, *_: (j, 0, 0, 0)),
        ),
        out_shape=jax.ShapeDtypeStruct((H, ZH, SENT, PAIR), BF16),
        compiler_params=pltpu.CompilerParams(vmem_limit_bytes=56 * 2**20),
        cost_estimate=cost(10**9, 4 * 10**6),
        name="pick",
    )(offsets_two, offsets_three, queries, keys, values)


def pack_kernel(q_ref, k_ref, v_ref, bulk_ref, rest_ref):
    bulk_ref[0, :, :PAIR] = q_ref[:, :PAIR]
    bulk_ref[0, :, PAIR : PAIR + WIDTH] = k_ref[...]
    bulk_ref[0, :, PAIR + WIDTH :] = v_ref[...]
    rest_ref[0] = q_ref[:, PAIR:]


def pack(queries, keys, values):
    block = pl.BlockSpec((ROWS, WIDTH), lambda j: (0, j))
    return pl.pallas_call(
        pack_kernel,
        grid=(GRP,),
        in_specs=[block] * 3,
        out_specs=[pl.BlockSpec((1, ROWS, columns), lambda j: (j, 0, 0)) for columns in (BULK, PAIR)],
        out_shape=[jax.ShapeDtypeStruct((GRP, ROWS, columns), BF16) for columns in (BULK, PAIR)],
        compiler_params=pltpu.CompilerParams(vmem_limit_bytes=56 * 2**20),
        cost_estimate=cost(0, 5 * 10**6),
        name="pack",
    )(queries, keys, values)


def compact_kernel(got_ref, out_ref):
    count, keys = ZH * H * LOCAL3, ZH * H * PICK
    row = iota((count, keys), 0)
    target = row // LOCAL3 * PICK + LOCAL2 + row % LOCAL3
    onehot = jnp.where(iota((count, keys), 1) == target, 1.0, 0.0).astype(BF16)
    chosen = jnp.dot(onehot, got_ref[:, :, :PICK, :].reshape(keys, PAIR), preferred_element_type=F32)
    out_ref[...] = chosen.astype(BF16)


def compact(got):
    return pl.pallas_call(
        compact_kernel,
        out_shape=jax.ShapeDtypeStruct((ZH * H * LOCAL3, PAIR), BF16),
        compiler_params=params(),
        cost_estimate=cost(10**8, 10**6),
        name="compact_three",
    )(got)


def sparse_kernel(place_ref, got_ref, far_ref, out_ref):
    low = iota((1, PAIR), 1) < HD
    one = jnp.ones((), BF16)
    near = got_ref[:, :, :PICK, :].reshape(ZH * H * PICK, PAIR)
    far = far_ref[...]
    half = PICK // 2
    raw = got_ref[:, pl.ds(place_ref[1], 1), PICK:, :].reshape(H * half, PAIR).astype(F32)
    head = jnp.where(low, raw, 0.0)
    tail = jnp.where(low, pltpu.roll(raw, HD, 1), 0.0).reshape(H, half, PAIR)
    tail_two = tail[:, : LOCAL2 - half].reshape(-1, PAIR)
    tail_three = tail[:, LOCAL2 - half :].reshape(-1, PAIR)

    def attend(q, kv, masked):
        scores = lax.dot_general(q.astype(BF16), kv, NT, preferred_element_type=F32)
        if masked:
            scores = jnp.where(iota((1, kv.shape[0]), 1) % PICK < LOCAL2, scores, -1e30)
        largest = jnp.max(scores, axis=-1, keepdims=True)
        expo = jnp.exp2((scores - largest) * SCALE2).astype(BF16)
        total = jnp.dot(expo, jnp.where(low, one, kv), preferred_element_type=F32)
        weight = total[:, :1]
        log_sum = largest * SCALE2 + jnp.log2(weight)
        top = log_sum.astype(BF16).astype(F32)
        middle = (log_sum - top).astype(BF16).astype(F32)
        rest = log_sum - top - middle
        lane = iota((1, PAIR), 1)
        stats = jnp.where(lane < 16, top, jnp.where(lane < 32, middle, rest))
        return jnp.where(low, stats, total / weight)

    rows = H * half // 2
    first = jnp.concatenate([attend(head[:rows], near, True), attend(head[rows:], near, True)], 0)
    first = first.reshape(GRP, XS, half, PAIR)
    second = attend(tail_two, near, True).reshape(GRP, XS, LOCAL2 - half, PAIR)
    third = attend(tail_three, far, False).reshape(GRP, XS, PICK - LOCAL2, PAIR)
    second = jnp.concatenate([second, third], axis=2)
    for x in range(XS):
        where = (x - place_ref[0] + XS) % XS
        out_ref[where, :, :half, :] = first[:, x].astype(BF16)
        out_ref[where, :, half:, :] = second[:, x].astype(BF16)


def sparse_levels(place, got, far):
    shape = (XS, GRP, PICK, PAIR)
    return pl.pallas_call(
        sparse_kernel,
        in_specs=[pl.BlockSpec(memory_space=pltpu.SMEM)] + [pl.BlockSpec(memory_space=pltpu.VMEM)] * 2,
        out_shape=jax.ShapeDtypeStruct(shape, BF16),
        compiler_params=params(),
        cost_estimate=cost(4 * 10**9, 2 * 10**6, 2 * 10**6),
        name="sparse_levels",
    )(place, got, far)


def dense_kernel(pair, scalar_ref, q_ref, bulk_ref, back_ref, out_ref, acc, top, aug, scores, few):
    zero, one = jnp.zeros((), BF16), jnp.ones((), BF16)
    blocks, parts = SEG1 // BLOCK, SEG1 // PART

    def mine(parity, rows):
        lane = iota((rows, PAIR), 1)
        return (lane >= HD) if parity else (lane < HD)

    def rows_of(block):
        return pl.ds(pl.multiple_of(block * BLOCK, BLOCK), BLOCK)

    keys = slice(PAIR + pair * PAIR, PAIR + (pair + 1) * PAIR)
    values = slice(keys.start + WIDTH, keys.stop + WIDTH)
    for parity in range(2):
        aug[parity] = jnp.where(mine(parity, SEG1), bulk_ref[:, values], one)

    def step(ahead, parity, largest, block):
        q, expected, total = None, None, None
        if ahead is not None:
            q = jnp.where(mine(ahead[0], BLOCK), q_ref[rows_of(ahead[1]), :PAIR], zero)
        for part in range(parts):
            lanes = slice(part * PART, (part + 1) * PART)
            if ahead is not None:
                fresh = lax.dot_general(q, bulk_ref[lanes, keys], NT, preferred_element_type=F32)
                scores[ahead[0], :, lanes] = fresh
                for i in range(0, PART, PAIR):
                    piece = fresh[:, i : i + PAIR]
                    expected = piece if expected is None else jnp.maximum(expected, piece)
            if parity is not None:
                expo = jnp.exp2((scores[parity, :, lanes] - largest) * SCALE2).astype(BF16)
                term = jnp.dot(expo, aug[parity, lanes, :], preferred_element_type=F32)
                total = term if total is None else total + term
        if parity is not None:
            acc[parity, rows_of(block), :] = total
            top[parity, rows_of(block), :] = jnp.broadcast_to(largest * SCALE2, (BLOCK, PAIR))
        if ahead is not None:
            return jnp.max(expected, axis=-1, keepdims=True)

    def level_one(block, largest):
        other = step((1, block), 0, largest, block)
        return step((0, jnp.minimum(block + 1, blocks - 1)), 1, other, block)

    lax.fori_loop(0, blocks, level_one, step((0, 0), None, None, None))

    for parity in range(2):
        head = pair * 2 + parity
        back = back_ref[(scalar_ref[0] - head + XS) % XS].astype(F32)

        def merge(rows, part, parity=parity):
            log_sum = part[:, 0:1] + part[:, 16:17] + part[:, 32:33]
            shaped = part if parity else pltpu.roll(part, HD, 1)
            shaped = jnp.where(mine(parity, part.shape[0]), shaped, 1.0)
            old = top[parity, rows, :]
            peak = jnp.maximum(old, log_sum)
            top[parity, rows, :] = peak
            acc[parity, rows, :] = acc[parity, rows, :] * jnp.exp2(old - peak) + shaped * jnp.exp2(log_sum - peak)

        merge(pl.ds(scalar_ref[1 + head], SEG1 // R2, stride=R2), back[:, :LOCAL2].reshape(SEG1 // R2, PAIR))
        for g in range(GRP):
            few[g * LOCAL3 : (g + 1) * LOCAL3, :] = back[g, LOCAL2 : LOCAL2 + LOCAL3]
        merge(pl.ds(scalar_ref[1 + OWN + head], SEG1 // R3, stride=R3), few[...])
    result = [acc[parity] / pltpu.roll(acc[parity], HD, 1) for parity in range(2)]
    out_ref[...] = jnp.where(mine(0, SEG1), result[0], result[1]).astype(BF16)


def dense_level(pair, scalars, q, bulk, back):
    return pl.pallas_call(
        functools.partial(dense_kernel, pair),
        in_specs=[pl.BlockSpec(memory_space=pltpu.SMEM)] + [pl.BlockSpec(memory_space=pltpu.VMEM)] * 3,
        out_shape=jax.ShapeDtypeStruct((SEG1, PAIR), BF16),
        scratch_shapes=[
            pltpu.VMEM((2, SEG1, PAIR), F32),
            pltpu.VMEM((2, SEG1, PAIR), F32),
            pltpu.VMEM((2, SEG1, PAIR), BF16),
            pltpu.VMEM((2, BLOCK, SEG1), F32),
            pltpu.VMEM((SEG1 // R3, PAIR), F32),
        ],
        compiler_params=params(),
        cost_estimate=cost(10 * 10**9, 2 * 10**6, 5 * 10**6),
        name="dense_level",
    )(scalars, q, bulk, back)


def project_kernel(place_ref, first_ref, second_ref, w_ref, out_ref):
    upper = place_ref[0] == 1
    part = WIDTH // (XS * ZH)
    columns = 512
    att = []
    for g in range(GRP):
        low, high = first_ref[g], second_ref[g]
        att.append(jnp.concatenate([jnp.where(upper, high, low), jnp.where(upper, low, high)], 1))
    for start in range(0, D, columns):
        total = None
        for g in range(GRP):
            rows = [g * WIDTH + (x * ZH + far) * part for far in range(ZH) for x in range(XS)]
            weights = jnp.concatenate([w_ref[row : row + part, start : start + columns] for row in rows], 0)
            term = jnp.dot(att[g], weights, preferred_element_type=F32)
            total = term if total is None else total + term
        out_ref[:, start : start + columns] = total.astype(BF16)


def project(zh, first, second, weights):
    return pl.pallas_call(
        project_kernel,
        in_specs=[pl.BlockSpec(memory_space=pltpu.SMEM)] + [pl.BlockSpec(memory_space=pltpu.VMEM)] * 3,
        out_shape=jax.ShapeDtypeStruct((ROWS, D), BF16),
        compiler_params=params(),
        cost_estimate=cost(2 * ROWS * D * D, 10 * 10**6),
        name="project",
    )(zh, first, second, weights)


def shift(value, axis, step):
    size = lax.axis_size(axis)
    return lax.ppermute(value, axis, [(i, (i + step) % size) for i in range(size)])


def after(value, *events):
    return lax.optimization_barrier((value, *events))[0]


def local(queries, keys, values, offsets_two, offsets_three, w_out):
    exchange = functools.partial(lax.all_to_all, axis_name=GROUP, split_axis=0, concat_axis=0, tiled=True)
    x, zh = lax.axis_index("x"), lax.axis_index("zh")
    first_head = lax.axis_index(GROUP) * OWN
    own_two = lax.dynamic_slice_in_dim(offsets_two, first_head, OWN)
    own_three = lax.dynamic_slice_in_dim(offsets_three, first_head, OWN)

    far_rows = shift(w_out, "zh", 1)
    small = pick(offsets_two, offsets_three, queries, keys, values)
    bulk, rest = pack(after(queries, small), keys, values)
    weights = jnp.concatenate([after(w_out, small), far_rows], 0)
    weights = lax.all_gather(weights, ("y", "x"), axis=0, tiled=True)
    got = lax.all_to_all(
        after(small, far_rows).reshape(H * ZH, SENT, PAIR), ("zl", "core", "x", "zh"), split_axis=0, concat_axis=0, tiled=True
    ).reshape(H, ZH, SENT, PAIR)

    bulk = exchange(after(bulk, got)).reshape(SEG1, BULK)
    far = lax.all_gather(compact(got), "y", axis=0, tiled=True)
    parts = sparse_levels(jnp.stack([x, zh]), got, far)
    back = jnp.stack([parts[0]] + [shift(parts[step], "x", step) for step in range(1, XS)])
    rest = exchange(after(rest, bulk, back)).reshape(SEG1, PAIR)
    scalars = jnp.concatenate([x.reshape(1), own_two, own_three])
    first = dense_level(0, scalars, bulk, bulk, back)
    first = exchange(after(first, rest).reshape(GRP, ROWS, PAIR))
    second = dense_level(1, scalars, rest, bulk, back)
    second = exchange(after(second, weights).reshape(GRP, ROWS, PAIR))
    return project(zh.reshape(1), first, second, weights)


def solution(mesh):
    rows = P(("y", "zh", "x", "zl", "core"), None)
    return jax.shard_map(
        local,
        mesh=fine_mesh(mesh),
        in_specs=(rows, rows, rows, P(), P(), P(("y", "zh", "x"), None)),
        out_specs=rows,
        check_vma=False,
    )
```

```python
import functools
import math

import jax
import jax.numpy as jnp
from jax import lax
from jax.experimental import pallas as pl
from jax.experimental.pallas import tpu as pltpu
from jax.sharding import Mesh
from jax.sharding import PartitionSpec as P

H = 32
HD = 64
PAIR = 2 * HD
R2 = 8
R3 = 64
D = H * HD
GRP = 8
XS = 4
ZH = 2
ROWS = 192
SEG1 = ROWS * GRP
OWN = H // GRP
WIDTH = OWN * HD
LOCAL2 = ROWS // R2
LOCAL3 = ROWS // R3
PICK = 32
SENT = PICK + PICK // 2
BLOCK = 512
PART = 256
BULK = PAIR + 2 * WIDTH
PER_STEP = 4
SCALE2 = HD**-0.5 * math.log2(math.e)
VMEM_LIMIT = 28 * 2**20
GROUP = ("zl", "core")
NT = (((1,), (1,)), ((), ()))
BF16 = jnp.bfloat16
F32 = jnp.float32


def fine_mesh(mesh):
    return Mesh(mesh.devices.reshape(4, 2, 8, 2, XS), ("zl", "core", "y", "zh", "x"))


def params():
    return pltpu.CompilerParams(vmem_limit_bytes=VMEM_LIMIT)


def cost(flops, traffic, transcendentals=0):
    return pl.CostEstimate(flops=flops, bytes_accessed=traffic, transcendentals=transcendentals)


def iota(shape, dim):
    return lax.broadcasted_iota(jnp.int32, shape, dim)


def pick_kernel(two_ref, three_ref, q_ref, k_ref, v_ref, small_ref):
    for group in range(PER_STEP):
        pick_group(group, two_ref, three_ref, q_ref, k_ref, v_ref, small_ref)


def pick_group(group, two_ref, three_ref, q_ref, k_ref, v_ref, small_ref):
    step = pl.program_id(0) * PER_STEP + group
    columns = slice(group * WIDTH, (group + 1) * WIDTH)
    row = iota((OWN * PICK, ROWS), 0)
    place = row % PICK
    target = jnp.full((OWN * PICK, ROWS), -1, jnp.int32)
    for i in range(OWN):
        two = place * R2 + two_ref[step * OWN + i]
        three = (place - LOCAL2) * R3 + three_ref[step * OWN + i]
        own = jnp.where(place < LOCAL2, two, jnp.where(place < LOCAL2 + LOCAL3, three, -1))
        target = jnp.where(row // PICK == i, own, target)
    onehot = jnp.where(iota((OWN * PICK, ROWS), 1) == target, 1.0, 0.0).astype(BF16)
    picked = [jnp.dot(onehot, ref[:, columns], preferred_element_type=F32) for ref in (q_ref, k_ref, v_ref)]
    low = iota((PICK, PAIR), 1) < HD
    for i in range(OWN):
        rows, lanes = slice(i * PICK, (i + 1) * PICK), slice(i // 2 * PAIR, (i // 2 + 1) * PAIR)
        q, k, v = (part[rows, lanes] for part in picked)
        if i % 2:
            k = pltpu.roll(k, HD, 1)
            head, tail = pltpu.roll(q[: PICK // 2], HD, 1), q[PICK // 2 :]
        else:
            v = pltpu.roll(v, HD, 1)
            head, tail = q[: PICK // 2], pltpu.roll(q[PICK // 2 :], HD, 1)
        kv = jnp.where(low, k, v).astype(BF16)
        lines = jnp.where(low[: PICK // 2], head, tail).astype(BF16)
        for zh in range(ZH):
            small_ref[group * OWN + i, zh, :PICK, :] = kv
            small_ref[group * OWN + i, zh, PICK:, :] = lines


def pick(offsets_two, offsets_three, queries, keys, values):
    block = pl.BlockSpec((ROWS, PER_STEP * WIDTH), lambda j, *_: (0, j))
    return pl.pallas_call(
        pick_kernel,
        grid_spec=pltpu.PrefetchScalarGridSpec(
            num_scalar_prefetch=2,
            grid=(GRP // PER_STEP,),
            in_specs=[block] * 3,
            out_specs=pl.BlockSpec((PER_STEP * OWN, ZH, SENT, PAIR), lambda j, *_: (j, 0, 0, 0)),
        ),
        out_shape=jax.ShapeDtypeStruct((H, ZH, SENT, PAIR), BF16),
        compiler_params=pltpu.CompilerParams(vmem_limit_bytes=56 * 2**20),
        cost_estimate=cost(10**9, 4 * 10**6),
        name="pick",
    )(offsets_two, offsets_three, queries, keys, values)


def pack_queries_kernel(q_ref, out_ref):
    for g in range(GRP):
        out_ref[g] = q_ref[:, g * WIDTH + PAIR : (g + 1) * WIDTH]


def pack_queries(queries):
    return pl.pallas_call(
        pack_queries_kernel,
        out_shape=jax.ShapeDtypeStruct((GRP, ROWS, PAIR), BF16),
        compiler_params=pltpu.CompilerParams(vmem_limit_bytes=56 * 2**20),
        cost_estimate=cost(0, 10**6),
        name="pack_queries",
    )(queries)


def pack_kernel(q_ref, k_ref, v_ref, out_ref):
    out_ref[0, :, :PAIR] = q_ref[:, :PAIR]
    out_ref[0, :, PAIR : PAIR + WIDTH] = k_ref[...]
    out_ref[0, :, PAIR + WIDTH :] = v_ref[...]


def pack(queries, keys, values):
    block = pl.BlockSpec((ROWS, WIDTH), lambda j: (0, j))
    return pl.pallas_call(
        pack_kernel,
        grid=(GRP,),
        in_specs=[block] * 3,
        out_specs=pl.BlockSpec((1, ROWS, BULK), lambda j: (j, 0, 0)),
        out_shape=jax.ShapeDtypeStruct((GRP, ROWS, BULK), BF16),
        compiler_params=pltpu.CompilerParams(vmem_limit_bytes=56 * 2**20),
        cost_estimate=cost(0, 4 * 10**6),
        name="pack",
    )(queries, keys, values)


def compact_kernel(got_ref, out_ref):
    count, keys = ZH * H * LOCAL3, ZH * H * PICK
    row = iota((count, keys), 0)
    target = row // LOCAL3 * PICK + LOCAL2 + row % LOCAL3
    onehot = jnp.where(iota((count, keys), 1) == target, 1.0, 0.0).astype(BF16)
    chosen = jnp.dot(onehot, got_ref[:, :, :PICK, :].reshape(keys, PAIR), preferred_element_type=F32)
    out_ref[...] = chosen.astype(BF16)


def compact(got):
    return pl.pallas_call(
        compact_kernel,
        out_shape=jax.ShapeDtypeStruct((ZH * H * LOCAL3, PAIR), BF16),
        compiler_params=params(),
        cost_estimate=cost(10**8, 10**6),
        name="compact_three",
    )(got)


def sparse_kernel(place_ref, got_ref, far_ref, out_ref):
    low = iota((1, PAIR), 1) < HD
    one = jnp.ones((), BF16)
    near = got_ref[:, :, :PICK, :].reshape(ZH * H * PICK, PAIR)
    far = far_ref[...]
    half = PICK // 2
    raw = got_ref[:, pl.ds(place_ref[1], 1), PICK:, :].reshape(H * half, PAIR).astype(F32)
    head = jnp.where(low, raw, 0.0)
    tail = jnp.where(low, pltpu.roll(raw, HD, 1), 0.0).reshape(H, half, PAIR)
    tail_two = tail[:, : LOCAL2 - half].reshape(-1, PAIR)
    tail_three = tail[:, LOCAL2 - half :].reshape(-1, PAIR)

    def attend(q, kv, masked):
        scores = lax.dot_general(q.astype(BF16), kv, NT, preferred_element_type=F32)
        if masked:
            scores = jnp.where(iota((1, kv.shape[0]), 1) % PICK < LOCAL2, scores, -1e30)
        largest = jnp.max(scores, axis=-1, keepdims=True)
        expo = jnp.exp2((scores - largest) * SCALE2).astype(BF16)
        total = jnp.dot(expo, jnp.where(low, one, kv), preferred_element_type=F32)
        weight = total[:, :1]
        log_sum = largest * SCALE2 + jnp.log2(weight)
        top = log_sum.astype(BF16).astype(F32)
        middle = (log_sum - top).astype(BF16).astype(F32)
        rest = log_sum - top - middle
        lane = iota((1, PAIR), 1)
        stats = jnp.where(lane < 16, top, jnp.where(lane < 32, middle, rest))
        return jnp.where(low, stats, total / weight)

    rows = H * half // 2
    first = jnp.concatenate([attend(head[:rows], near, True), attend(head[rows:], near, True)], 0)
    first = first.reshape(GRP, XS, half, PAIR)
    second = attend(tail_two, near, True).reshape(GRP, XS, LOCAL2 - half, PAIR)
    third = attend(tail_three, far, False).reshape(GRP, XS, PICK - LOCAL2, PAIR)
    second = jnp.concatenate([second, third], axis=2)
    for x in range(XS):
        where = (x - place_ref[0] + XS) % XS
        out_ref[where, :, :half, :] = first[:, x].astype(BF16)
        out_ref[where, :, half:, :] = second[:, x].astype(BF16)


def sparse_levels(place, got, far):
    shape = (XS, GRP, PICK, PAIR)
    return pl.pallas_call(
        sparse_kernel,
        in_specs=[pl.BlockSpec(memory_space=pltpu.SMEM)] + [pl.BlockSpec(memory_space=pltpu.VMEM)] * 2,
        out_shape=jax.ShapeDtypeStruct(shape, BF16),
        compiler_params=params(),
        cost_estimate=cost(4 * 10**9, 2 * 10**6, 2 * 10**6),
        name="sparse_levels",
    )(place, got, far)


def dense_kernel(pair, scalar_ref, q_ref, bulk_ref, back_ref, out_ref, acc, top, aug, scores, few):
    zero, one = jnp.zeros((), BF16), jnp.ones((), BF16)
    blocks, parts = SEG1 // BLOCK, SEG1 // PART

    def mine(parity, rows):
        lane = iota((rows, PAIR), 1)
        return (lane >= HD) if parity else (lane < HD)

    def rows_of(block):
        return pl.ds(pl.multiple_of(block * BLOCK, BLOCK), BLOCK)

    keys = slice(PAIR + pair * PAIR, PAIR + (pair + 1) * PAIR)
    values = slice(keys.start + WIDTH, keys.stop + WIDTH)
    for parity in range(2):
        aug[parity] = jnp.where(mine(parity, SEG1), bulk_ref[:, values], one)

    def step(ahead, parity, largest, block):
        q, expected, total = None, None, None
        if ahead is not None:
            q = jnp.where(mine(ahead[0], BLOCK), q_ref[rows_of(ahead[1]), :PAIR], zero)
        for part in range(parts):
            lanes = slice(part * PART, (part + 1) * PART)
            if ahead is not None:
                fresh = lax.dot_general(q, bulk_ref[lanes, keys], NT, preferred_element_type=F32)
                scores[ahead[0], :, lanes] = fresh
                for i in range(0, PART, PAIR):
                    piece = fresh[:, i : i + PAIR]
                    expected = piece if expected is None else jnp.maximum(expected, piece)
            if parity is not None:
                expo = jnp.exp2((scores[parity, :, lanes] - largest) * SCALE2).astype(BF16)
                term = jnp.dot(expo, aug[parity, lanes, :], preferred_element_type=F32)
                total = term if total is None else total + term
        if parity is not None:
            acc[parity, rows_of(block), :] = total
            top[parity, rows_of(block), :] = jnp.broadcast_to(largest * SCALE2, (BLOCK, PAIR))
        if ahead is not None:
            return jnp.max(expected, axis=-1, keepdims=True)

    def level_one(block, largest):
        other = step((1, block), 0, largest, block)
        return step((0, jnp.minimum(block + 1, blocks - 1)), 1, other, block)

    lax.fori_loop(0, blocks, level_one, step((0, 0), None, None, None))

    for parity in range(2):
        head = pair * 2 + parity
        back = back_ref[(scalar_ref[0] - head + XS) % XS].astype(F32)

        def merge(rows, part, parity=parity):
            log_sum = part[:, 0:1] + part[:, 16:17] + part[:, 32:33]
            shaped = part if parity else pltpu.roll(part, HD, 1)
            shaped = jnp.where(mine(parity, part.shape[0]), shaped, 1.0)
            old = top[parity, rows, :]
            peak = jnp.maximum(old, log_sum)
            top[parity, rows, :] = peak
            acc[parity, rows, :] = acc[parity, rows, :] * jnp.exp2(old - peak) + shaped * jnp.exp2(log_sum - peak)

        merge(pl.ds(scalar_ref[1 + head], SEG1 // R2, stride=R2), back[:, :LOCAL2].reshape(SEG1 // R2, PAIR))
        for g in range(GRP):
            few[g * LOCAL3 : (g + 1) * LOCAL3, :] = back[g, LOCAL2 : LOCAL2 + LOCAL3]
        merge(pl.ds(scalar_ref[1 + OWN + head], SEG1 // R3, stride=R3), few[...])
    result = [acc[parity] / pltpu.roll(acc[parity], HD, 1) for parity in range(2)]
    out_ref[...] = jnp.where(mine(0, SEG1), result[0], result[1]).astype(BF16)


def dense_level(pair, scalars, q, bulk, back):
    return pl.pallas_call(
        functools.partial(dense_kernel, pair),
        in_specs=[pl.BlockSpec(memory_space=pltpu.SMEM)] + [pl.BlockSpec(memory_space=pltpu.VMEM)] * 3,
        out_shape=jax.ShapeDtypeStruct((SEG1, PAIR), BF16),
        scratch_shapes=[
            pltpu.VMEM((2, SEG1, PAIR), F32),
            pltpu.VMEM((2, SEG1, PAIR), F32),
            pltpu.VMEM((2, SEG1, PAIR), BF16),
            pltpu.VMEM((2, BLOCK, SEG1), F32),
            pltpu.VMEM((SEG1 // R3, PAIR), F32),
        ],
        compiler_params=params(),
        cost_estimate=cost(10 * 10**9, 2 * 10**6, 5 * 10**6),
        name="dense_level",
    )(scalars, q, bulk, back)


def project_kernel(pair, place_ref, att_ref, w_ref, *refs):
    out_ref = refs[-1]
    far = (place_ref[0] + pair) % ZH
    part = WIDTH // (XS * ZH)
    columns = 512
    for start in range(0, D, columns):
        lanes = slice(start, start + columns)
        total = refs[0][:, lanes] if pair else None
        for first in range(0, GRP, 2):
            both = (first, first + 1)
            rows = [pl.multiple_of(g * WIDTH + x * ZH * part + far * part, part) for g in both for x in range(XS)]
            weights = jnp.concatenate([w_ref[pl.ds(row, part), lanes] for row in rows], 0)
            att = jnp.concatenate([att_ref[g] for g in both], 1)
            term = jnp.dot(att, weights, preferred_element_type=F32)
            total = term if total is None else total + term
        out_ref[:, lanes] = total.astype(out_ref.dtype)


def project(pair, zh, att, weights, *before):
    return pl.pallas_call(
        functools.partial(project_kernel, pair),
        in_specs=[pl.BlockSpec(memory_space=pltpu.SMEM)] + [pl.BlockSpec(memory_space=pltpu.VMEM)] * (2 + pair),
        out_shape=jax.ShapeDtypeStruct((ROWS, D), BF16 if pair else F32),
        compiler_params=params(),
        cost_estimate=cost(ROWS * D * D, 6 * 10**6),
        name="project",
    )(zh, att, weights, *before)


def shift(value, axis, step):
    size = lax.axis_size(axis)
    return lax.ppermute(value, axis, [(i, (i + step) % size) for i in range(size)])


def after(value, *events):
    return lax.optimization_barrier((value, *events))[0]


def local(queries, keys, values, offsets_two, offsets_three, w_out):
    exchange = functools.partial(lax.all_to_all, axis_name=GROUP, split_axis=0, concat_axis=0, tiled=True)
    x, zh = lax.axis_index("x"), lax.axis_index("zh")
    first_head = lax.axis_index(GROUP) * OWN
    own_two = lax.dynamic_slice_in_dim(offsets_two, first_head, OWN)
    own_three = lax.dynamic_slice_in_dim(offsets_three, first_head, OWN)

    rest = pack_queries(queries)
    far_rows = shift(after(w_out, rest), "zh", 1)
    small = pick(offsets_two, offsets_three, after(queries, rest), keys, values)
    weights = jnp.concatenate([after(w_out, small), far_rows], 0)
    weights = lax.all_gather(weights, ("y", "x"), axis=0, tiled=True)
    rest = exchange(rest).reshape(SEG1, PAIR)
    got = lax.all_to_all(
        after(small, far_rows, rest).reshape(H * ZH, SENT, PAIR),
        ("zl", "core", "x", "zh"),
        split_axis=0,
        concat_axis=0,
        tiled=True,
    ).reshape(H, ZH, SENT, PAIR)
    bulk = pack(after(queries, small), keys, values)

    bulk = exchange(after(bulk, got)).reshape(SEG1, BULK)
    far = lax.all_gather(compact(got), "y", axis=0, tiled=True)
    parts = sparse_levels(jnp.stack([x, zh]), got, far)
    back = jnp.stack([parts[0]] + [shift(parts[step], "x", step) for step in range(1, XS)])
    scalars = jnp.concatenate([x.reshape(1), own_two, own_three])
    first = dense_level(0, scalars, bulk, bulk, back)
    first = exchange(first.reshape(GRP, ROWS, PAIR))
    second = dense_level(1, scalars, rest, bulk, back)
    second = exchange(second.reshape(GRP, ROWS, PAIR))
    place = zh.reshape(1)
    return project(1, place, second, weights, project(0, place, first, weights))


def solution(mesh):
    rows = P(("y", "zh", "x", "zl", "core"), None)
    return jax.shard_map(
        local,
        mesh=fine_mesh(mesh),
        in_specs=(rows, rows, rows, P(), P(), P(("y", "zh", "x"), None)),
        out_specs=rows,
        check_vma=False,
    )
```

```python
import functools
import math

import jax
import jax.numpy as jnp
from jax import lax
from jax.experimental import pallas as pl
from jax.experimental.pallas import tpu as pltpu
from jax.sharding import Mesh
from jax.sharding import PartitionSpec as P

H = 32
HD = 64
PAIR = 2 * HD
R2 = 8
R3 = 64
D = H * HD
GRP = 8
XS = 4
ZH = 2
ROWS = 192
SEG1 = ROWS * GRP
OWN = H // GRP
WIDTH = OWN * HD
LOCAL2 = ROWS // R2
LOCAL3 = ROWS // R3
PICK = 32
SENT = PICK + PICK // 2
BLOCK = 512
PART = 256
BULK = PAIR + 2 * WIDTH
PER_STEP = 4
SCALE2 = HD**-0.5 * math.log2(math.e)
VMEM_LIMIT = 28 * 2**20
GROUP = ("zl", "core")
NT = (((1,), (1,)), ((), ()))
BF16 = jnp.bfloat16
F32 = jnp.float32


def fine_mesh(mesh):
    return Mesh(mesh.devices.reshape(4, 2, 8, 2, XS), ("zl", "core", "y", "zh", "x"))


def params():
    return pltpu.CompilerParams(vmem_limit_bytes=VMEM_LIMIT)


def cost(flops, traffic, transcendentals=0):
    return pl.CostEstimate(flops=flops, bytes_accessed=traffic, transcendentals=transcendentals)


def iota(shape, dim):
    return lax.broadcasted_iota(jnp.int32, shape, dim)


def pick_kernel(two_ref, three_ref, q_ref, k_ref, v_ref, small_ref):
    for group in range(PER_STEP):
        pick_group(group, two_ref, three_ref, q_ref, k_ref, v_ref, small_ref)


def pick_group(group, two_ref, three_ref, q_ref, k_ref, v_ref, small_ref):
    step = pl.program_id(0) * PER_STEP + group
    columns = slice(group * WIDTH, (group + 1) * WIDTH)
    row = iota((OWN * PICK, ROWS), 0)
    place = row % PICK
    target = jnp.full((OWN * PICK, ROWS), -1, jnp.int32)
    for i in range(OWN):
        two = place * R2 + two_ref[step * OWN + i]
        three = (place - LOCAL2) * R3 + three_ref[step * OWN + i]
        own = jnp.where(place < LOCAL2, two, jnp.where(place < LOCAL2 + LOCAL3, three, -1))
        target = jnp.where(row // PICK == i, own, target)
    onehot = jnp.where(iota((OWN * PICK, ROWS), 1) == target, 1.0, 0.0).astype(BF16)
    picked = [jnp.dot(onehot, ref[:, columns], preferred_element_type=F32) for ref in (q_ref, k_ref, v_ref)]
    low = iota((PICK, PAIR), 1) < HD
    for i in range(OWN):
        rows, lanes = slice(i * PICK, (i + 1) * PICK), slice(i // 2 * PAIR, (i // 2 + 1) * PAIR)
        q, k, v = (part[rows, lanes] for part in picked)
        if i % 2:
            k = pltpu.roll(k, HD, 1)
            head, tail = pltpu.roll(q[: PICK // 2], HD, 1), q[PICK // 2 :]
        else:
            v = pltpu.roll(v, HD, 1)
            head, tail = q[: PICK // 2], pltpu.roll(q[PICK // 2 :], HD, 1)
        kv = jnp.where(low, k, v).astype(BF16)
        lines = jnp.where(low[: PICK // 2], head, tail).astype(BF16)
        for zh in range(ZH):
            small_ref[group * OWN + i, zh, :PICK, :] = kv
            small_ref[group * OWN + i, zh, PICK:, :] = lines


def pick(offsets_two, offsets_three, queries, keys, values):
    block = pl.BlockSpec((ROWS, PER_STEP * WIDTH), lambda j, *_: (0, j))
    return pl.pallas_call(
        pick_kernel,
        grid_spec=pltpu.PrefetchScalarGridSpec(
            num_scalar_prefetch=2,
            grid=(GRP // PER_STEP,),
            in_specs=[block] * 3,
            out_specs=pl.BlockSpec((PER_STEP * OWN, ZH, SENT, PAIR), lambda j, *_: (j, 0, 0, 0)),
        ),
        out_shape=jax.ShapeDtypeStruct((H, ZH, SENT, PAIR), BF16),
        compiler_params=pltpu.CompilerParams(vmem_limit_bytes=56 * 2**20),
        cost_estimate=cost(10**9, 4 * 10**6),
        name="pick",
    )(offsets_two, offsets_three, queries, keys, values)


def pack_kernel(q_ref, k_ref, v_ref, bulk_ref, rest_ref):
    bulk_ref[0, :, :PAIR] = q_ref[:, :PAIR]
    bulk_ref[0, :, PAIR : PAIR + WIDTH] = k_ref[...]
    bulk_ref[0, :, PAIR + WIDTH :] = v_ref[...]
    rest_ref[0] = q_ref[:, PAIR:]


def pack(queries, keys, values):
    block = pl.BlockSpec((ROWS, WIDTH), lambda j: (0, j))
    return pl.pallas_call(
        pack_kernel,
        grid=(GRP,),
        in_specs=[block] * 3,
        out_specs=[pl.BlockSpec((1, ROWS, columns), lambda j: (j, 0, 0)) for columns in (BULK, PAIR)],
        out_shape=[jax.ShapeDtypeStruct((GRP, ROWS, columns), BF16) for columns in (BULK, PAIR)],
        compiler_params=pltpu.CompilerParams(vmem_limit_bytes=56 * 2**20),
        cost_estimate=cost(0, 5 * 10**6),
        name="pack",
    )(queries, keys, values)


def compact_kernel(got_ref, out_ref):
    count, keys = ZH * H * LOCAL3, ZH * H * PICK
    row = iota((count, keys), 0)
    target = row // LOCAL3 * PICK + LOCAL2 + row % LOCAL3
    onehot = jnp.where(iota((count, keys), 1) == target, 1.0, 0.0).astype(BF16)
    chosen = jnp.dot(onehot, got_ref[:, :, :PICK, :].reshape(keys, PAIR), preferred_element_type=F32)
    out_ref[...] = chosen.astype(BF16)


def compact(got):
    return pl.pallas_call(
        compact_kernel,
        out_shape=jax.ShapeDtypeStruct((ZH * H * LOCAL3, PAIR), BF16),
        compiler_params=params(),
        cost_estimate=cost(10**8, 10**6),
        name="compact_three",
    )(got)


def sparse_kernel(place_ref, got_ref, far_ref, out_ref):
    low = iota((1, PAIR), 1) < HD
    one = jnp.ones((), BF16)
    near = got_ref[:, :, :PICK, :].reshape(ZH * H * PICK, PAIR)
    far = far_ref[...]
    half = PICK // 2
    raw = got_ref[:, pl.ds(place_ref[1], 1), PICK:, :].reshape(H * half, PAIR).astype(F32)
    head = jnp.where(low, raw, 0.0)
    tail = jnp.where(low, pltpu.roll(raw, HD, 1), 0.0).reshape(H, half, PAIR)
    tail_two = tail[:, : LOCAL2 - half].reshape(-1, PAIR)
    tail_three = tail[:, LOCAL2 - half :].reshape(-1, PAIR)

    def attend(q, kv, masked):
        scores = lax.dot_general(q.astype(BF16), kv, NT, preferred_element_type=F32)
        if masked:
            scores = jnp.where(iota((1, kv.shape[0]), 1) % PICK < LOCAL2, scores, -1e30)
        largest = jnp.max(scores, axis=-1, keepdims=True)
        expo = jnp.exp2((scores - largest) * SCALE2).astype(BF16)
        total = jnp.dot(expo, jnp.where(low, one, kv), preferred_element_type=F32)
        weight = total[:, :1]
        log_sum = largest * SCALE2 + jnp.log2(weight)
        top = log_sum.astype(BF16).astype(F32)
        middle = (log_sum - top).astype(BF16).astype(F32)
        rest = log_sum - top - middle
        lane = iota((1, PAIR), 1)
        stats = jnp.where(lane < 16, top, jnp.where(lane < 32, middle, rest))
        return jnp.where(low, stats, total / weight)

    rows = H * half // 2
    first = jnp.concatenate([attend(head[:rows], near, True), attend(head[rows:], near, True)], 0)
    first = first.reshape(GRP, XS, half, PAIR)
    second = attend(tail_two, near, True).reshape(GRP, XS, LOCAL2 - half, PAIR)
    third = attend(tail_three, far, False).reshape(GRP, XS, PICK - LOCAL2, PAIR)
    second = jnp.concatenate([second, third], axis=2)
    for x in range(XS):
        where = (x - place_ref[0] + XS) % XS
        out_ref[where, :, :half, :] = first[:, x].astype(BF16)
        out_ref[where, :, half:, :] = second[:, x].astype(BF16)


def sparse_levels(place, got, far):
    shape = (XS, GRP, PICK, PAIR)
    return pl.pallas_call(
        sparse_kernel,
        in_specs=[pl.BlockSpec(memory_space=pltpu.SMEM)] + [pl.BlockSpec(memory_space=pltpu.VMEM)] * 2,
        out_shape=jax.ShapeDtypeStruct(shape, BF16),
        compiler_params=params(),
        cost_estimate=cost(4 * 10**9, 2 * 10**6, 2 * 10**6),
        name="sparse_levels",
    )(place, got, far)


def dense_kernel(pair, scalar_ref, q_ref, bulk_ref, back_ref, out_ref, acc, top, aug, scores, few):
    zero, one = jnp.zeros((), BF16), jnp.ones((), BF16)
    blocks, parts = SEG1 // BLOCK, SEG1 // PART

    def mine(parity, rows):
        lane = iota((rows, PAIR), 1)
        return (lane >= HD) if parity else (lane < HD)

    def rows_of(block):
        return pl.ds(pl.multiple_of(block * BLOCK, BLOCK), BLOCK)

    keys = slice(PAIR + pair * PAIR, PAIR + (pair + 1) * PAIR)
    values = slice(keys.start + WIDTH, keys.stop + WIDTH)
    for parity in range(2):
        aug[parity] = jnp.where(mine(parity, SEG1), bulk_ref[:, values], one)

    def step(ahead, parity, largest, block):
        q, expected, total = None, None, None
        if ahead is not None:
            q = jnp.where(mine(ahead[0], BLOCK), q_ref[rows_of(ahead[1]), :PAIR], zero)
        for part in range(parts):
            lanes = slice(part * PART, (part + 1) * PART)
            if ahead is not None:
                fresh = lax.dot_general(q, bulk_ref[lanes, keys], NT, preferred_element_type=F32)
                scores[ahead[0], :, lanes] = fresh
                for i in range(0, PART, PAIR):
                    piece = fresh[:, i : i + PAIR]
                    expected = piece if expected is None else jnp.maximum(expected, piece)
            if parity is not None:
                expo = jnp.exp2((scores[parity, :, lanes] - largest) * SCALE2).astype(BF16)
                term = jnp.dot(expo, aug[parity, lanes, :], preferred_element_type=F32)
                total = term if total is None else total + term
        if parity is not None:
            acc[parity, rows_of(block), :] = total
            top[parity, rows_of(block), :] = jnp.broadcast_to(largest * SCALE2, (BLOCK, PAIR))
        if ahead is not None:
            return jnp.max(expected, axis=-1, keepdims=True)

    def level_one(block, largest):
        other = step((1, block), 0, largest, block)
        return step((0, jnp.minimum(block + 1, blocks - 1)), 1, other, block)

    lax.fori_loop(0, blocks, level_one, step((0, 0), None, None, None))

    for parity in range(2):
        head = pair * 2 + parity
        back = back_ref[(scalar_ref[0] - head + XS) % XS].astype(F32)

        def merge(rows, part, parity=parity):
            log_sum = part[:, 0:1] + part[:, 16:17] + part[:, 32:33]
            shaped = part if parity else pltpu.roll(part, HD, 1)
            shaped = jnp.where(mine(parity, part.shape[0]), shaped, 1.0)
            old = top[parity, rows, :]
            peak = jnp.maximum(old, log_sum)
            top[parity, rows, :] = peak
            acc[parity, rows, :] = acc[parity, rows, :] * jnp.exp2(old - peak) + shaped * jnp.exp2(log_sum - peak)

        merge(pl.ds(scalar_ref[1 + head], SEG1 // R2, stride=R2), back[:, :LOCAL2].reshape(SEG1 // R2, PAIR))
        for g in range(GRP):
            few[g * LOCAL3 : (g + 1) * LOCAL3, :] = back[g, LOCAL2 : LOCAL2 + LOCAL3]
        merge(pl.ds(scalar_ref[1 + OWN + head], SEG1 // R3, stride=R3), few[...])
    result = [acc[parity] / pltpu.roll(acc[parity], HD, 1) for parity in range(2)]
    out_ref[...] = jnp.where(mine(0, SEG1), result[0], result[1]).astype(BF16)


def dense_level(pair, scalars, q, bulk, back):
    return pl.pallas_call(
        functools.partial(dense_kernel, pair),
        in_specs=[pl.BlockSpec(memory_space=pltpu.SMEM)] + [pl.BlockSpec(memory_space=pltpu.VMEM)] * 3,
        out_shape=jax.ShapeDtypeStruct((SEG1, PAIR), BF16),
        scratch_shapes=[
            pltpu.VMEM((2, SEG1, PAIR), F32),
            pltpu.VMEM((2, SEG1, PAIR), F32),
            pltpu.VMEM((2, SEG1, PAIR), BF16),
            pltpu.VMEM((2, BLOCK, SEG1), F32),
            pltpu.VMEM((SEG1 // R3, PAIR), F32),
        ],
        compiler_params=params(),
        cost_estimate=cost(10 * 10**9, 2 * 10**6, 5 * 10**6),
        name="dense_level",
    )(scalars, q, bulk, back)


COLUMNS = 512
PART_ROWS = WIDTH // (XS * ZH)


def pairs_of_groups(att_ref):
    for first in range(0, GRP, 2):
        yield first, jnp.concatenate([att_ref[first], att_ref[first + 1]], 1)


def project_first_kernel(place_ref, att_ref, w_ref, out_ref, later_ref):
    def weights_of(first, half, lanes):
        far = (place_ref[0] + half) % ZH
        both = (first, first + 1)
        rows = [pl.multiple_of(g * WIDTH + (x * ZH + far) * PART_ROWS, PART_ROWS) for g in both for x in range(XS)]
        return jnp.concatenate([w_ref[pl.ds(row, PART_ROWS), lanes] for row in rows], 0)

    for start in range(0, D, COLUMNS):
        lanes = slice(start, start + COLUMNS)
        total = None
        for first, att in pairs_of_groups(att_ref):
            term = jnp.dot(att, weights_of(first, 0, lanes), preferred_element_type=F32)
            total = term if total is None else total + term
            later_ref[first * PAIR : (first + 2) * PAIR, lanes] = weights_of(first, 1, lanes)
        out_ref[:, lanes] = total


def project_first(zh, att, weights):
    return pl.pallas_call(
        project_first_kernel,
        in_specs=[pl.BlockSpec(memory_space=pltpu.SMEM)] + [pl.BlockSpec(memory_space=pltpu.VMEM)] * 2,
        out_specs=[pl.BlockSpec(memory_space=pltpu.VMEM)] * 2,
        out_shape=[jax.ShapeDtypeStruct((ROWS, D), F32), jax.ShapeDtypeStruct((D // 2, D), BF16)],
        compiler_params=params(),
        cost_estimate=cost(ROWS * D * D, 12 * 10**6),
        name="project_first",
    )(zh, att, weights)


def project_second_kernel(before_ref, att_ref, w_ref, out_ref):
    for start in range(0, D, COLUMNS):
        lanes = slice(start, start + COLUMNS)
        total = before_ref[:, lanes]
        for first, att in pairs_of_groups(att_ref):
            total += jnp.dot(att, w_ref[first * PAIR : (first + 2) * PAIR, lanes], preferred_element_type=F32)
        out_ref[:, lanes] = total.astype(BF16)


def project_second(before, att, weights):
    return pl.pallas_call(
        project_second_kernel,
        in_specs=[pl.BlockSpec(memory_space=pltpu.VMEM)] * 3,
        out_specs=pl.BlockSpec(memory_space=pltpu.VMEM),
        out_shape=jax.ShapeDtypeStruct((ROWS, D), BF16),
        compiler_params=params(),
        cost_estimate=cost(ROWS * D * D, 6 * 10**6),
        name="project_second",
    )(before, att, weights)


def shift(value, axis, step):
    size = lax.axis_size(axis)
    return lax.ppermute(value, axis, [(i, (i + step) % size) for i in range(size)])


def after(value, *events):
    return lax.optimization_barrier((value, *events))[0]


def local(queries, keys, values, offsets_two, offsets_three, w_out):
    exchange = functools.partial(lax.all_to_all, axis_name=GROUP, split_axis=0, concat_axis=0, tiled=True)
    x, zh = lax.axis_index("x"), lax.axis_index("zh")
    first_head = lax.axis_index(GROUP) * OWN
    own_two = lax.dynamic_slice_in_dim(offsets_two, first_head, OWN)
    own_three = lax.dynamic_slice_in_dim(offsets_three, first_head, OWN)

    far_rows = shift(w_out, "zh", 1)
    small = pick(offsets_two, offsets_three, queries, keys, values)
    bulk, rest = pack(after(queries, small), keys, values)
    weights = jnp.concatenate([after(w_out, small), far_rows], 0)
    weights = lax.all_gather(weights, ("y", "x"), axis=0, tiled=True)
    got = lax.all_to_all(
        after(small, far_rows).reshape(H * ZH, SENT, PAIR), ("zl", "core", "x", "zh"), split_axis=0, concat_axis=0, tiled=True
    ).reshape(H, ZH, SENT, PAIR)

    bulk = exchange(after(bulk, got)).reshape(SEG1, BULK)
    far = lax.all_gather(compact(got), "y", axis=0, tiled=True)
    parts = sparse_levels(jnp.stack([x, zh]), got, far)
    back = jnp.stack([parts[0]] + [shift(parts[step], "x", step) for step in range(1, XS)])
    rest = exchange(after(rest, bulk, back)).reshape(SEG1, PAIR)
    scalars = jnp.concatenate([x.reshape(1), own_two, own_three])
    first = dense_level(0, scalars, bulk, bulk, back)
    first = exchange(after(first, rest).reshape(GRP, ROWS, PAIR))
    second = dense_level(1, scalars, rest, bulk, back)
    second = exchange(after(second, first).reshape(GRP, ROWS, PAIR))
    partial, weights = project_first(zh.reshape(1), first, weights)
    return project_second(partial, second, weights)


def solution(mesh):
    rows = P(("y", "zh", "x", "zl", "core"), None)
    return jax.shard_map(
        local,
        mesh=fine_mesh(mesh),
        in_specs=(rows, rows, rows, P(), P(), P(("y", "zh", "x"), None)),
        out_specs=rows,
        check_vma=False,
    )
```

```python
import functools
import math

import jax
import jax.numpy as jnp
from jax import lax
from jax.experimental import pallas as pl
from jax.experimental.pallas import tpu as pltpu
from jax.sharding import Mesh
from jax.sharding import PartitionSpec as P

H = 32
HD = 64
PAIR = 2 * HD
R2 = 8
R3 = 64
D = H * HD
GRP = 8
XS = 4
ZH = 2
ROWS = 192
SEG1 = ROWS * GRP
OWN = H // GRP
WIDTH = OWN * HD
LOCAL2 = ROWS // R2
LOCAL3 = ROWS // R3
PICK = 32
SENT = PICK + PICK // 2
BLOCK = 512
PART = 256
BULK = PAIR + 2 * WIDTH
PER_STEP = 4
SCALE2 = HD**-0.5 * math.log2(math.e)
VMEM_LIMIT = 28 * 2**20
GROUP = ("zl", "core")
NT = (((1,), (1,)), ((), ()))
BF16 = jnp.bfloat16
F32 = jnp.float32


def fine_mesh(mesh):
    return Mesh(mesh.devices.reshape(4, 2, 8, 2, XS), ("zl", "core", "y", "zh", "x"))


def params():
    return pltpu.CompilerParams(vmem_limit_bytes=VMEM_LIMIT)


def cost(flops, traffic, transcendentals=0):
    return pl.CostEstimate(flops=flops, bytes_accessed=traffic, transcendentals=transcendentals)


def iota(shape, dim):
    return lax.broadcasted_iota(jnp.int32, shape, dim)


def pick_kernel(two_ref, three_ref, q_ref, k_ref, v_ref, small_ref):
    for group in range(PER_STEP):
        pick_group(group, two_ref, three_ref, q_ref, k_ref, v_ref, small_ref)


def pick_group(group, two_ref, three_ref, q_ref, k_ref, v_ref, small_ref):
    step = pl.program_id(0) * PER_STEP + group
    columns = slice(group * WIDTH, (group + 1) * WIDTH)
    row = iota((OWN * PICK, ROWS), 0)
    place = row % PICK
    target = jnp.full((OWN * PICK, ROWS), -1, jnp.int32)
    for i in range(OWN):
        two = place * R2 + two_ref[step * OWN + i]
        three = (place - LOCAL2) * R3 + three_ref[step * OWN + i]
        own = jnp.where(place < LOCAL2, two, jnp.where(place < LOCAL2 + LOCAL3, three, -1))
        target = jnp.where(row // PICK == i, own, target)
    onehot = jnp.where(iota((OWN * PICK, ROWS), 1) == target, 1.0, 0.0).astype(BF16)
    picked = [jnp.dot(onehot, ref[:, columns], preferred_element_type=F32) for ref in (q_ref, k_ref, v_ref)]
    low = iota((PICK, PAIR), 1) < HD
    for i in range(OWN):
        rows, lanes = slice(i * PICK, (i + 1) * PICK), slice(i // 2 * PAIR, (i // 2 + 1) * PAIR)
        q, k, v = (part[rows, lanes] for part in picked)
        if i % 2:
            k = pltpu.roll(k, HD, 1)
            head, tail = pltpu.roll(q[: PICK // 2], HD, 1), q[PICK // 2 :]
        else:
            v = pltpu.roll(v, HD, 1)
            head, tail = q[: PICK // 2], pltpu.roll(q[PICK // 2 :], HD, 1)
        kv = jnp.where(low, k, v).astype(BF16)
        lines = jnp.where(low[: PICK // 2], head, tail).astype(BF16)
        for zh in range(ZH):
            small_ref[group * OWN + i, zh, :PICK, :] = kv
            small_ref[group * OWN + i, zh, PICK:, :] = lines


def pick(offsets_two, offsets_three, queries, keys, values):
    block = pl.BlockSpec((ROWS, PER_STEP * WIDTH), lambda j, *_: (0, j))
    return pl.pallas_call(
        pick_kernel,
        grid_spec=pltpu.PrefetchScalarGridSpec(
            num_scalar_prefetch=2,
            grid=(GRP // PER_STEP,),
            in_specs=[block] * 3,
            out_specs=pl.BlockSpec((PER_STEP * OWN, ZH, SENT, PAIR), lambda j, *_: (j, 0, 0, 0)),
        ),
        out_shape=jax.ShapeDtypeStruct((H, ZH, SENT, PAIR), BF16),
        compiler_params=pltpu.CompilerParams(vmem_limit_bytes=56 * 2**20),
        cost_estimate=cost(10**9, 4 * 10**6),
        name="pick",
    )(offsets_two, offsets_three, queries, keys, values)


def pack_kernel(q_ref, k_ref, v_ref, bulk_ref, rest_ref):
    bulk_ref[0, :, :PAIR] = q_ref[:, :PAIR]
    bulk_ref[0, :, PAIR : PAIR + WIDTH] = k_ref[...]
    bulk_ref[0, :, PAIR + WIDTH :] = v_ref[...]
    rest_ref[0] = q_ref[:, PAIR:]


def pack(queries, keys, values):
    block = pl.BlockSpec((ROWS, WIDTH), lambda j: (0, j))
    return pl.pallas_call(
        pack_kernel,
        grid=(GRP,),
        in_specs=[block] * 3,
        out_specs=[pl.BlockSpec((1, ROWS, columns), lambda j: (j, 0, 0)) for columns in (BULK, PAIR)],
        out_shape=[jax.ShapeDtypeStruct((GRP, ROWS, columns), BF16) for columns in (BULK, PAIR)],
        compiler_params=pltpu.CompilerParams(vmem_limit_bytes=56 * 2**20),
        cost_estimate=cost(0, 5 * 10**6),
        name="pack",
    )(queries, keys, values)


def compact_kernel(got_ref, out_ref):
    count, keys = ZH * H * LOCAL3, ZH * H * PICK
    row = iota((count, keys), 0)
    target = row // LOCAL3 * PICK + LOCAL2 + row % LOCAL3
    onehot = jnp.where(iota((count, keys), 1) == target, 1.0, 0.0).astype(BF16)
    chosen = jnp.dot(onehot, got_ref[:, :, :PICK, :].reshape(keys, PAIR), preferred_element_type=F32)
    out_ref[...] = chosen.astype(BF16)


def compact(got):
    return pl.pallas_call(
        compact_kernel,
        out_shape=jax.ShapeDtypeStruct((ZH * H * LOCAL3, PAIR), BF16),
        compiler_params=params(),
        cost_estimate=cost(10**8, 10**6),
        name="compact_three",
    )(got)


def sparse_kernel(place_ref, got_ref, far_ref, out_ref):
    low = iota((1, PAIR), 1) < HD
    one = jnp.ones((), BF16)
    near = got_ref[:, :, :PICK, :].reshape(ZH * H * PICK, PAIR)
    far = far_ref[...]
    half = PICK // 2
    raw = got_ref[:, pl.ds(place_ref[1], 1), PICK:, :].reshape(H * half, PAIR).astype(F32)
    head = jnp.where(low, raw, 0.0)
    tail = jnp.where(low, pltpu.roll(raw, HD, 1), 0.0).reshape(H, half, PAIR)
    tail_two = tail[:, : LOCAL2 - half].reshape(-1, PAIR)
    tail_three = tail[:, LOCAL2 - half :].reshape(-1, PAIR)

    def attend(q, kv, masked):
        scores = lax.dot_general(q.astype(BF16), kv, NT, preferred_element_type=F32)
        if masked:
            scores = jnp.where(iota((1, kv.shape[0]), 1) % PICK < LOCAL2, scores, -1e30)
        largest = jnp.max(scores, axis=-1, keepdims=True)
        expo = jnp.exp2((scores - largest) * SCALE2).astype(BF16)
        total = jnp.dot(expo, jnp.where(low, one, kv), preferred_element_type=F32)
        weight = total[:, :1]
        log_sum = largest * SCALE2 + jnp.log2(weight)
        top = log_sum.astype(BF16).astype(F32)
        middle = (log_sum - top).astype(BF16).astype(F32)
        rest = log_sum - top - middle
        lane = iota((1, PAIR), 1)
        stats = jnp.where(lane < 16, top, jnp.where(lane < 32, middle, rest))
        return jnp.where(low, stats, total / weight)

    rows = H * half // 2
    first = jnp.concatenate([attend(head[:rows], near, True), attend(head[rows:], near, True)], 0)
    first = first.reshape(GRP, XS, half, PAIR)
    second = attend(tail_two, near, True).reshape(GRP, XS, LOCAL2 - half, PAIR)
    third = attend(tail_three, far, False).reshape(GRP, XS, PICK - LOCAL2, PAIR)
    second = jnp.concatenate([second, third], axis=2)
    for x in range(XS):
        where = (x - place_ref[0] + XS) % XS
        out_ref[where, :, :half, :] = first[:, x].astype(BF16)
        out_ref[where, :, half:, :] = second[:, x].astype(BF16)


def sparse_levels(place, got, far):
    shape = (XS, GRP, PICK, PAIR)
    return pl.pallas_call(
        sparse_kernel,
        in_specs=[pl.BlockSpec(memory_space=pltpu.SMEM)] + [pl.BlockSpec(memory_space=pltpu.VMEM)] * 2,
        out_shape=jax.ShapeDtypeStruct(shape, BF16),
        compiler_params=params(),
        cost_estimate=cost(4 * 10**9, 2 * 10**6, 2 * 10**6),
        name="sparse_levels",
    )(place, got, far)


def dense_kernel(pair, scalar_ref, q_ref, bulk_ref, back_ref, out_ref, acc, top, aug, scores, few):
    zero, one = jnp.zeros((), BF16), jnp.ones((), BF16)
    blocks, parts = SEG1 // BLOCK, SEG1 // PART

    def mine(parity, rows):
        lane = iota((rows, PAIR), 1)
        return (lane >= HD) if parity else (lane < HD)

    def rows_of(block):
        return pl.ds(pl.multiple_of(block * BLOCK, BLOCK), BLOCK)

    keys = slice(PAIR + pair * PAIR, PAIR + (pair + 1) * PAIR)
    values = slice(keys.start + WIDTH, keys.stop + WIDTH)
    for parity in range(2):
        aug[parity] = jnp.where(mine(parity, SEG1), bulk_ref[:, values], one)

    def step(ahead, parity, largest, block):
        q, expected, total = None, None, None
        if ahead is not None:
            q = jnp.where(mine(ahead[0], BLOCK), q_ref[rows_of(ahead[1]), :PAIR], zero)
        for part in range(parts):
            lanes = slice(part * PART, (part + 1) * PART)
            if ahead is not None:
                fresh = lax.dot_general(q, bulk_ref[lanes, keys], NT, preferred_element_type=F32)
                scores[ahead[0], :, lanes] = fresh
                for i in range(0, PART, PAIR):
                    piece = fresh[:, i : i + PAIR]
                    expected = piece if expected is None else jnp.maximum(expected, piece)
            if parity is not None:
                expo = jnp.exp2((scores[parity, :, lanes] - largest) * SCALE2).astype(BF16)
                term = jnp.dot(expo, aug[parity, lanes, :], preferred_element_type=F32)
                total = term if total is None else total + term
        if parity is not None:
            acc[parity, rows_of(block), :] = total
            top[parity, rows_of(block), :] = jnp.broadcast_to(largest * SCALE2, (BLOCK, PAIR))
        if ahead is not None:
            return jnp.max(expected, axis=-1, keepdims=True)

    def level_one(block, largest):
        other = step((1, block), 0, largest, block)
        return step((0, jnp.minimum(block + 1, blocks - 1)), 1, other, block)

    lax.fori_loop(0, blocks, level_one, step((0, 0), None, None, None))

    for parity in range(2):
        head = pair * 2 + parity
        back = back_ref[(scalar_ref[0] - head + XS) % XS].astype(F32)

        def merge(rows, part, parity=parity):
            log_sum = part[:, 0:1] + part[:, 16:17] + part[:, 32:33]
            shaped = part if parity else pltpu.roll(part, HD, 1)
            shaped = jnp.where(mine(parity, part.shape[0]), shaped, 1.0)
            old = top[parity, rows, :]
            peak = jnp.maximum(old, log_sum)
            top[parity, rows, :] = peak
            acc[parity, rows, :] = acc[parity, rows, :] * jnp.exp2(old - peak) + shaped * jnp.exp2(log_sum - peak)

        merge(pl.ds(scalar_ref[1 + head], SEG1 // R2, stride=R2), back[:, :LOCAL2].reshape(SEG1 // R2, PAIR))
        for g in range(GRP):
            few[g * LOCAL3 : (g + 1) * LOCAL3, :] = back[g, LOCAL2 : LOCAL2 + LOCAL3]
        merge(pl.ds(scalar_ref[1 + OWN + head], SEG1 // R3, stride=R3), few[...])
    result = [acc[parity] / pltpu.roll(acc[parity], HD, 1) for parity in range(2)]
    out_ref[...] = jnp.where(mine(0, SEG1), result[0], result[1]).astype(BF16)


def dense_level(pair, scalars, q, bulk, back):
    return pl.pallas_call(
        functools.partial(dense_kernel, pair),
        in_specs=[pl.BlockSpec(memory_space=pltpu.SMEM)] + [pl.BlockSpec(memory_space=pltpu.VMEM)] * 3,
        out_shape=jax.ShapeDtypeStruct((SEG1, PAIR), BF16),
        scratch_shapes=[
            pltpu.VMEM((2, SEG1, PAIR), F32),
            pltpu.VMEM((2, SEG1, PAIR), F32),
            pltpu.VMEM((2, SEG1, PAIR), BF16),
            pltpu.VMEM((2, BLOCK, SEG1), F32),
            pltpu.VMEM((SEG1 // R3, PAIR), F32),
        ],
        compiler_params=params(),
        cost_estimate=cost(10 * 10**9, 2 * 10**6, 5 * 10**6),
        name="dense_level",
    )(scalars, q, bulk, back)


COLUMNS = 512
PART_ROWS = WIDTH // (XS * ZH)


def pairs_of_groups(att_ref):
    for first in range(0, GRP, 2):
        yield first, jnp.concatenate([att_ref[first], att_ref[first + 1]], 1)


def project_first_kernel(place_ref, att_ref, w_ref, out_ref, later_ref):
    def weights_of(first, half, lanes):
        far = (place_ref[0] + half) % ZH
        both = (first, first + 1)
        rows = [pl.multiple_of(g * WIDTH + (x * ZH + far) * PART_ROWS, PART_ROWS) for g in both for x in range(XS)]
        return jnp.concatenate([w_ref[pl.ds(row, PART_ROWS), lanes] for row in rows], 0)

    for start in range(0, D, COLUMNS):
        lanes = slice(start, start + COLUMNS)
        total = None
        for first, att in pairs_of_groups(att_ref):
            term = jnp.dot(att, weights_of(first, 0, lanes), preferred_element_type=F32)
            total = term if total is None else total + term
            later_ref[first * PAIR : (first + 2) * PAIR, lanes] = weights_of(first, 1, lanes)
        out_ref[:, lanes] = total


def project_first(zh, att, weights):
    return pl.pallas_call(
        project_first_kernel,
        in_specs=[pl.BlockSpec(memory_space=pltpu.SMEM)] + [pl.BlockSpec(memory_space=pltpu.VMEM)] * 2,
        out_specs=[pl.BlockSpec(memory_space=pltpu.VMEM)] * 2,
        out_shape=[jax.ShapeDtypeStruct((ROWS, D), F32), jax.ShapeDtypeStruct((D // 2, D), BF16)],
        compiler_params=params(),
        cost_estimate=cost(ROWS * D * D, 12 * 10**6),
        name="project_first",
    )(zh, att, weights)


def project_second_kernel(before_ref, att_ref, w_ref, out_ref, total):
    step = pl.program_id(0)

    @pl.when(step == 0)
    def _():
        total[...] = before_ref[...]

    att = jnp.concatenate([att_ref[0], att_ref[1]], 1)
    for start in range(0, D, COLUMNS):
        lanes = slice(start, start + COLUMNS)
        total[:, lanes] += jnp.dot(att, w_ref[:, lanes], preferred_element_type=F32)

    @pl.when(step == pl.num_programs(0) - 1)
    def _():
        out_ref[...] = total[...].astype(BF16)


def project_second(before, att, weights):
    return pl.pallas_call(
        project_second_kernel,
        grid=(GRP // 2,),
        in_specs=[
            pl.BlockSpec((ROWS, D), lambda j: (0, 0)),
            pl.BlockSpec((2, ROWS, PAIR), lambda j: (j, 0, 0)),
            pl.BlockSpec((2 * PAIR, D), lambda j: (j, 0)),
        ],
        out_specs=pl.BlockSpec((ROWS, D), lambda j: (0, 0)),
        out_shape=jax.ShapeDtypeStruct((ROWS, D), BF16),
        scratch_shapes=[pltpu.VMEM((ROWS, D), F32)],
        compiler_params=pltpu.CompilerParams(vmem_limit_bytes=56 * 2**20),
        cost_estimate=cost(ROWS * D * D, 6 * 10**6),
        name="project_second",
    )(before, att, weights)


def shift(value, axis, step):
    size = lax.axis_size(axis)
    return lax.ppermute(value, axis, [(i, (i + step) % size) for i in range(size)])


def after(value, *events):
    return lax.optimization_barrier((value, *events))[0]


def local(queries, keys, values, offsets_two, offsets_three, w_out):
    exchange = functools.partial(lax.all_to_all, axis_name=GROUP, split_axis=0, concat_axis=0, tiled=True)
    x, zh = lax.axis_index("x"), lax.axis_index("zh")
    first_head = lax.axis_index(GROUP) * OWN
    own_two = lax.dynamic_slice_in_dim(offsets_two, first_head, OWN)
    own_three = lax.dynamic_slice_in_dim(offsets_three, first_head, OWN)

    far_rows = shift(w_out, "zh", 1)
    small = pick(offsets_two, offsets_three, queries, keys, values)
    bulk, rest = pack(after(queries, small), keys, values)
    weights = jnp.concatenate([after(w_out, small), far_rows], 0)
    weights = lax.all_gather(weights, ("y", "x"), axis=0, tiled=True)
    got = lax.all_to_all(
        after(small, far_rows).reshape(H * ZH, SENT, PAIR), ("zl", "core", "x", "zh"), split_axis=0, concat_axis=0, tiled=True
    ).reshape(H, ZH, SENT, PAIR)

    bulk = exchange(after(bulk, got)).reshape(SEG1, BULK)
    far = lax.all_gather(compact(got), "y", axis=0, tiled=True)
    parts = sparse_levels(jnp.stack([x, zh]), got, far)
    back = jnp.stack([parts[0]] + [shift(parts[step], "x", step) for step in range(1, XS)])
    rest = exchange(after(rest, bulk, back)).reshape(SEG1, PAIR)
    scalars = jnp.concatenate([x.reshape(1), own_two, own_three])
    first = dense_level(0, scalars, bulk, bulk, back)
    first = exchange(after(first, rest).reshape(GRP, ROWS, PAIR))
    second = dense_level(1, scalars, rest, bulk, back)
    second = exchange(after(second, first).reshape(GRP, ROWS, PAIR))
    partial, weights = project_first(zh.reshape(1), first, weights)
    return project_second(partial, second, weights)


def solution(mesh):
    rows = P(("y", "zh", "x", "zl", "core"), None)
    return jax.shard_map(
        local,
        mesh=fine_mesh(mesh),
        in_specs=(rows, rows, rows, P(), P(), P(("y", "zh", "x"), None)),
        out_specs=rows,
        check_vma=False,
    )
```

```python
import functools
import math

import jax
import jax.numpy as jnp
from jax import lax
from jax.experimental import pallas as pl
from jax.experimental.pallas import tpu as pltpu
from jax.sharding import Mesh
from jax.sharding import PartitionSpec as P

H = 32
HD = 64
PAIR = 2 * HD
R2 = 8
R3 = 64
D = H * HD
GRP = 8
XS = 4
ZH = 2
ROWS = 192
SEG1 = ROWS * GRP
OWN = H // GRP
WIDTH = OWN * HD
LOCAL2 = ROWS // R2
LOCAL3 = ROWS // R3
PICK = 32
SENT = PICK + PICK // 2
BLOCK = 512
PART = 256
BULK = PAIR + 2 * WIDTH
PER_STEP = 4
SCALE2 = HD**-0.5 * math.log2(math.e)
VMEM_LIMIT = 28 * 2**20
GROUP = ("zl", "core")
NT = (((1,), (1,)), ((), ()))
BF16 = jnp.bfloat16
F32 = jnp.float32


def fine_mesh(mesh):
    return Mesh(mesh.devices.reshape(4, 2, 8, 2, XS), ("zl", "core", "y", "zh", "x"))


def params():
    return pltpu.CompilerParams(vmem_limit_bytes=VMEM_LIMIT)


def cost(flops, traffic, transcendentals=0):
    return pl.CostEstimate(flops=flops, bytes_accessed=traffic, transcendentals=transcendentals)


def iota(shape, dim):
    return lax.broadcasted_iota(jnp.int32, shape, dim)


def pick_kernel(two_ref, three_ref, q_ref, k_ref, v_ref, small_ref):
    for group in range(PER_STEP):
        pick_group(group, two_ref, three_ref, q_ref, k_ref, v_ref, small_ref)


def pick_group(group, two_ref, three_ref, q_ref, k_ref, v_ref, small_ref):
    step = pl.program_id(0) * PER_STEP + group
    columns = slice(group * WIDTH, (group + 1) * WIDTH)
    row = iota((OWN * PICK, ROWS), 0)
    place = row % PICK
    target = jnp.full((OWN * PICK, ROWS), -1, jnp.int32)
    for i in range(OWN):
        two = place * R2 + two_ref[step * OWN + i]
        three = (place - LOCAL2) * R3 + three_ref[step * OWN + i]
        own = jnp.where(place < LOCAL2, two, jnp.where(place < LOCAL2 + LOCAL3, three, -1))
        target = jnp.where(row // PICK == i, own, target)
    onehot = jnp.where(iota((OWN * PICK, ROWS), 1) == target, 1.0, 0.0).astype(BF16)
    picked = [jnp.dot(onehot, ref[:, columns], preferred_element_type=F32) for ref in (q_ref, k_ref, v_ref)]
    low = iota((PICK, PAIR), 1) < HD
    for i in range(OWN):
        rows, lanes = slice(i * PICK, (i + 1) * PICK), slice(i // 2 * PAIR, (i // 2 + 1) * PAIR)
        q, k, v = (part[rows, lanes] for part in picked)
        if i % 2:
            k = pltpu.roll(k, HD, 1)
            head, tail = pltpu.roll(q[: PICK // 2], HD, 1), q[PICK // 2 :]
        else:
            v = pltpu.roll(v, HD, 1)
            head, tail = q[: PICK // 2], pltpu.roll(q[PICK // 2 :], HD, 1)
        kv = jnp.where(low, k, v).astype(BF16)
        lines = jnp.where(low[: PICK // 2], head, tail).astype(BF16)
        for zh in range(ZH):
            small_ref[group * OWN + i, zh, :PICK, :] = kv
            small_ref[group * OWN + i, zh, PICK:, :] = lines


def pick(offsets_two, offsets_three, queries, keys, values):
    block = pl.BlockSpec((ROWS, PER_STEP * WIDTH), lambda j, *_: (0, j))
    return pl.pallas_call(
        pick_kernel,
        grid_spec=pltpu.PrefetchScalarGridSpec(
            num_scalar_prefetch=2,
            grid=(GRP // PER_STEP,),
            in_specs=[block] * 3,
            out_specs=pl.BlockSpec((PER_STEP * OWN, ZH, SENT, PAIR), lambda j, *_: (j, 0, 0, 0)),
        ),
        out_shape=jax.ShapeDtypeStruct((H, ZH, SENT, PAIR), BF16),
        compiler_params=pltpu.CompilerParams(vmem_limit_bytes=56 * 2**20),
        cost_estimate=cost(10**9, 4 * 10**6),
        name="pick",
    )(offsets_two, offsets_three, queries, keys, values)


def pack_kernel(q_ref, k_ref, v_ref, bulk_ref, rest_ref):
    bulk_ref[0, :, :PAIR] = q_ref[:, :PAIR]
    bulk_ref[0, :, PAIR : PAIR + WIDTH] = k_ref[...]
    bulk_ref[0, :, PAIR + WIDTH :] = v_ref[...]
    rest_ref[0] = q_ref[:, PAIR:]


def pack(queries, keys, values):
    block = pl.BlockSpec((ROWS, WIDTH), lambda j: (0, j))
    return pl.pallas_call(
        pack_kernel,
        grid=(GRP,),
        in_specs=[block] * 3,
        out_specs=[pl.BlockSpec((1, ROWS, columns), lambda j: (j, 0, 0)) for columns in (BULK, PAIR)],
        out_shape=[jax.ShapeDtypeStruct((GRP, ROWS, columns), BF16) for columns in (BULK, PAIR)],
        compiler_params=pltpu.CompilerParams(vmem_limit_bytes=56 * 2**20),
        cost_estimate=cost(0, 5 * 10**6),
        name="pack",
    )(queries, keys, values)


def compact_kernel(got_ref, out_ref):
    count, keys = ZH * H * LOCAL3, ZH * H * PICK
    row = iota((count, keys), 0)
    target = row // LOCAL3 * PICK + LOCAL2 + row % LOCAL3
    onehot = jnp.where(iota((count, keys), 1) == target, 1.0, 0.0).astype(BF16)
    chosen = jnp.dot(onehot, got_ref[:, :, :PICK, :].reshape(keys, PAIR), preferred_element_type=F32)
    out_ref[...] = chosen.astype(BF16)


def compact(got):
    return pl.pallas_call(
        compact_kernel,
        out_shape=jax.ShapeDtypeStruct((ZH * H * LOCAL3, PAIR), BF16),
        compiler_params=params(),
        cost_estimate=cost(10**8, 10**6),
        name="compact_three",
    )(got)


def sparse_kernel(place_ref, got_ref, far_ref, out_ref):
    low = iota((1, PAIR), 1) < HD
    one = jnp.ones((), BF16)
    near = got_ref[:, :, :PICK, :].reshape(ZH * H * PICK, PAIR)
    far = far_ref[...]
    half = PICK // 2
    raw = got_ref[:, pl.ds(place_ref[1], 1), PICK:, :].reshape(H * half, PAIR).astype(F32)
    head = jnp.where(low, raw, 0.0)
    tail = jnp.where(low, pltpu.roll(raw, HD, 1), 0.0).reshape(H, half, PAIR)
    tail_two = tail[:, : LOCAL2 - half].reshape(-1, PAIR)
    tail_three = tail[:, LOCAL2 - half :].reshape(-1, PAIR)

    def attend(q, kv, masked):
        scores = lax.dot_general(q.astype(BF16), kv, NT, preferred_element_type=F32)
        if masked:
            scores = jnp.where(iota((1, kv.shape[0]), 1) % PICK < LOCAL2, scores, -1e30)
        largest = jnp.max(scores, axis=-1, keepdims=True)
        expo = jnp.exp2((scores - largest) * SCALE2).astype(BF16)
        total = jnp.dot(expo, jnp.where(low, one, kv), preferred_element_type=F32)
        weight = total[:, :1]
        log_sum = largest * SCALE2 + jnp.log2(weight)
        top = log_sum.astype(BF16).astype(F32)
        middle = (log_sum - top).astype(BF16).astype(F32)
        rest = log_sum - top - middle
        lane = iota((1, PAIR), 1)
        stats = jnp.where(lane < 16, top, jnp.where(lane < 32, middle, rest))
        return jnp.where(low, stats, total / weight)

    rows = H * half // 2
    first = jnp.concatenate([attend(head[:rows], near, True), attend(head[rows:], near, True)], 0)
    first = first.reshape(GRP, XS, half, PAIR)
    second = attend(tail_two, near, True).reshape(GRP, XS, LOCAL2 - half, PAIR)
    third = attend(tail_three, far, False).reshape(GRP, XS, PICK - LOCAL2, PAIR)
    second = jnp.concatenate([second, third], axis=2)
    for x in range(XS):
        where = (x - place_ref[0] + XS) % XS
        out_ref[where, :, :half, :] = first[:, x].astype(BF16)
        out_ref[where, :, half:, :] = second[:, x].astype(BF16)


def sparse_levels(place, got, far):
    shape = (XS, GRP, PICK, PAIR)
    return pl.pallas_call(
        sparse_kernel,
        in_specs=[pl.BlockSpec(memory_space=pltpu.SMEM)] + [pl.BlockSpec(memory_space=pltpu.VMEM)] * 2,
        out_shape=jax.ShapeDtypeStruct(shape, BF16),
        compiler_params=params(),
        cost_estimate=cost(4 * 10**9, 2 * 10**6, 2 * 10**6),
        name="sparse_levels",
    )(place, got, far)


def dense_kernel(pair, scalar_ref, q_ref, bulk_ref, back_ref, out_ref, acc, top, aug, scores, few):
    zero, one = jnp.zeros((), BF16), jnp.ones((), BF16)
    blocks, parts = SEG1 // BLOCK, SEG1 // PART

    def mine(parity, rows):
        lane = iota((rows, PAIR), 1)
        return (lane >= HD) if parity else (lane < HD)

    def rows_of(block):
        return pl.ds(pl.multiple_of(block * BLOCK, BLOCK), BLOCK)

    keys = slice(PAIR + pair * PAIR, PAIR + (pair + 1) * PAIR)
    values = slice(keys.start + WIDTH, keys.stop + WIDTH)
    for parity in range(2):
        aug[parity] = jnp.where(mine(parity, SEG1), bulk_ref[:, values], one)

    def step(ahead, parity, largest, block):
        q, expected, total = None, None, None
        if ahead is not None:
            q = jnp.where(mine(ahead[0], BLOCK), q_ref[rows_of(ahead[1]), :PAIR], zero)
        for part in range(parts):
            lanes = slice(part * PART, (part + 1) * PART)
            if ahead is not None:
                fresh = lax.dot_general(q, bulk_ref[lanes, keys], NT, preferred_element_type=F32)
                scores[ahead[0], :, lanes] = fresh
                for i in range(0, PART, PAIR):
                    piece = fresh[:, i : i + PAIR]
                    expected = piece if expected is None else jnp.maximum(expected, piece)
            if parity is not None:
                expo = jnp.exp2((scores[parity, :, lanes] - largest) * SCALE2).astype(BF16)
                term = jnp.dot(expo, aug[parity, lanes, :], preferred_element_type=F32)
                total = term if total is None else total + term
        if parity is not None:
            acc[parity, rows_of(block), :] = total
            top[parity, rows_of(block), :] = jnp.broadcast_to(largest * SCALE2, (BLOCK, PAIR))
        if ahead is not None:
            return jnp.max(expected, axis=-1, keepdims=True)

    def level_one(block, largest):
        other = step((1, block), 0, largest, block)
        return step((0, jnp.minimum(block + 1, blocks - 1)), 1, other, block)

    lax.fori_loop(0, blocks, level_one, step((0, 0), None, None, None))

    for parity in range(2):
        head = pair * 2 + parity
        back = back_ref[(scalar_ref[0] - head + XS) % XS].astype(F32)

        def merge(rows, part, parity=parity):
            log_sum = part[:, 0:1] + part[:, 16:17] + part[:, 32:33]
            shaped = part if parity else pltpu.roll(part, HD, 1)
            shaped = jnp.where(mine(parity, part.shape[0]), shaped, 1.0)
            old = top[parity, rows, :]
            peak = jnp.maximum(old, log_sum)
            top[parity, rows, :] = peak
            acc[parity, rows, :] = acc[parity, rows, :] * jnp.exp2(old - peak) + shaped * jnp.exp2(log_sum - peak)

        merge(pl.ds(scalar_ref[1 + head], SEG1 // R2, stride=R2), back[:, :LOCAL2].reshape(SEG1 // R2, PAIR))
        for g in range(GRP):
            few[g * LOCAL3 : (g + 1) * LOCAL3, :] = back[g, LOCAL2 : LOCAL2 + LOCAL3]
        merge(pl.ds(scalar_ref[1 + OWN + head], SEG1 // R3, stride=R3), few[...])
    result = [acc[parity] / pltpu.roll(acc[parity], HD, 1) for parity in range(2)]
    out_ref[...] = jnp.where(mine(0, SEG1), result[0], result[1]).astype(BF16)


def dense_level(pair, scalars, q, bulk, back):
    return pl.pallas_call(
        functools.partial(dense_kernel, pair),
        in_specs=[pl.BlockSpec(memory_space=pltpu.SMEM)] + [pl.BlockSpec(memory_space=pltpu.VMEM)] * 3,
        out_shape=jax.ShapeDtypeStruct((SEG1, PAIR), BF16),
        scratch_shapes=[
            pltpu.VMEM((2, SEG1, PAIR), F32),
            pltpu.VMEM((2, SEG1, PAIR), F32),
            pltpu.VMEM((2, SEG1, PAIR), BF16),
            pltpu.VMEM((2, BLOCK, SEG1), F32),
            pltpu.VMEM((SEG1 // R3, PAIR), F32),
        ],
        compiler_params=params(),
        cost_estimate=cost(10 * 10**9, 2 * 10**6, 5 * 10**6),
        name="dense_level",
    )(scalars, q, bulk, back)


COLUMNS = 512
PART_ROWS = WIDTH // (XS * ZH)


def pairs_of_groups(att_ref):
    for first in range(0, GRP, 2):
        yield first, jnp.concatenate([att_ref[first], att_ref[first + 1]], 1)


def project_first_kernel(place_ref, att_ref, w_ref, out_ref, later_ref):
    def weights_of(first, half, lanes):
        far = (place_ref[0] + half) % ZH
        both = (first, first + 1)
        rows = [pl.multiple_of(g * WIDTH + (x * ZH + far) * PART_ROWS, PART_ROWS) for g in both for x in range(XS)]
        return jnp.concatenate([w_ref[pl.ds(row, PART_ROWS), lanes] for row in rows], 0)

    for start in range(0, D, COLUMNS):
        lanes = slice(start, start + COLUMNS)
        total = None
        for first, att in pairs_of_groups(att_ref):
            term = jnp.dot(att, weights_of(first, 0, lanes), preferred_element_type=F32)
            total = term if total is None else total + term
            later_ref[first * PAIR : (first + 2) * PAIR, lanes] = weights_of(first, 1, lanes)
        out_ref[:, lanes] = total


def project_first(zh, att, weights):
    return pl.pallas_call(
        project_first_kernel,
        in_specs=[pl.BlockSpec(memory_space=pltpu.SMEM)] + [pl.BlockSpec(memory_space=pltpu.VMEM)] * 2,
        out_specs=[pl.BlockSpec(memory_space=pltpu.VMEM)] * 2,
        out_shape=[jax.ShapeDtypeStruct((ROWS, D), F32), jax.ShapeDtypeStruct((D // 2, D), BF16)],
        compiler_params=params(),
        cost_estimate=cost(ROWS * D * D, 12 * 10**6),
        name="project_first",
    )(zh, att, weights)


def project_second_kernel(before_ref, att_ref, w_ref, out_ref):
    total = before_ref[...]
    for first, att in pairs_of_groups(att_ref):
        total += jnp.dot(att, w_ref[first * PAIR : (first + 2) * PAIR, :], preferred_element_type=F32)
    out_ref[...] = total.astype(BF16)


def project_second(before, att, weights):
    columns = pl.BlockSpec((ROWS, COLUMNS), lambda j: (0, j))
    return pl.pallas_call(
        project_second_kernel,
        grid=(D // COLUMNS,),
        in_specs=[
            columns,
            pl.BlockSpec((GRP, ROWS, PAIR), lambda j: (0, 0, 0)),
            pl.BlockSpec((D // 2, COLUMNS), lambda j: (0, j)),
        ],
        out_specs=columns,
        out_shape=jax.ShapeDtypeStruct((ROWS, D), BF16),
        compiler_params=pltpu.CompilerParams(vmem_limit_bytes=56 * 2**20),
        cost_estimate=cost(ROWS * D * D, 6 * 10**6),
        name="project_second",
    )(before, att, weights)


def shift(value, axis, step):
    size = lax.axis_size(axis)
    return lax.ppermute(value, axis, [(i, (i + step) % size) for i in range(size)])


def after(value, *events):
    return lax.optimization_barrier((value, *events))[0]


def local(queries, keys, values, offsets_two, offsets_three, w_out):
    exchange = functools.partial(lax.all_to_all, axis_name=GROUP, split_axis=0, concat_axis=0, tiled=True)
    x, zh = lax.axis_index("x"), lax.axis_index("zh")
    first_head = lax.axis_index(GROUP) * OWN
    own_two = lax.dynamic_slice_in_dim(offsets_two, first_head, OWN)
    own_three = lax.dynamic_slice_in_dim(offsets_three, first_head, OWN)

    far_rows = shift(w_out, "zh", 1)
    small = pick(offsets_two, offsets_three, queries, keys, values)
    bulk, rest = pack(after(queries, small), keys, values)
    weights = jnp.concatenate([after(w_out, small), far_rows], 0)
    weights = lax.all_gather(weights, ("y", "x"), axis=0, tiled=True)
    got = lax.all_to_all(
        after(small, far_rows).reshape(H * ZH, SENT, PAIR), ("zl", "core", "x", "zh"), split_axis=0, concat_axis=0, tiled=True
    ).reshape(H, ZH, SENT, PAIR)

    bulk = exchange(after(bulk, got)).reshape(SEG1, BULK)
    far = lax.all_gather(compact(got), "y", axis=0, tiled=True)
    parts = sparse_levels(jnp.stack([x, zh]), got, far)
    back = jnp.stack([parts[0]] + [shift(parts[step], "x", step) for step in range(1, XS)])
    rest = exchange(after(rest, bulk, back)).reshape(SEG1, PAIR)
    scalars = jnp.concatenate([x.reshape(1), own_two, own_three])
    first = dense_level(0, scalars, bulk, bulk, back)
    first = exchange(after(first, rest).reshape(GRP, ROWS, PAIR))
    second = dense_level(1, scalars, rest, bulk, back)
    second = exchange(after(second, first).reshape(GRP, ROWS, PAIR))
    partial, weights = project_first(zh.reshape(1), first, weights)
    return project_second(partial, second, weights)


def solution(mesh):
    rows = P(("y", "zh", "x", "zl", "core"), None)
    return jax.shard_map(
        local,
        mesh=fine_mesh(mesh),
        in_specs=(rows, rows, rows, P(), P(), P(("y", "zh", "x"), None)),
        out_specs=rows,
        check_vma=False,
    )
```
